768 devices in a mesh: dom: 24 (over z, core), feat: 32 (over y, x).
Axes of the slice: x: 4, y: 8, z: 12, core: 2. Of those that a mesh axis runs over, the one named last changes fastest.
Arguments:
- features: bfloat16 [512, 24576], P('feat', 'dom'), may hold values from -6 to 6
- self_weight: bfloat16 [512, 512], P(None, 'feat'), may hold values from -0.25 to 0.25
- neigh_weight: bfloat16 [512, 512], P(None, 'feat'), may hold values from -0.25 to 0.25
- cotangent: bfloat16 [512, 24576], P('feat', 'dom'), may hold values from -6 to 6
- neighbours: int32 [24576, 16], P('dom'), may hold values from 0 to 1279
- degrees: int32 [24576], P('dom'), may hold values from 1 to 16
- send_rows: int32 [48, 128], P('dom'), may hold values from 0 to 1023
- send_count: int32 [48], P('dom'), may hold values from 32 to 128, as said below
Outputs:
- activated: bfloat16 [512, 24576], P('feat', 'dom')
- grad_x: float32 [512, 24576], P('feat', 'dom')
- grad_self: float32 [512, 512], P(None, 'feat')
- grad_neigh: float32 [512, 512], P(None, 'feat')
The draws below stay inside these ranges and needn't reach their ends.
Inputs may be any that keep to these rules, and one draw needn't show every extreme that they name: `neighbours`: indices into the extended rows of the node's partition: its 1024 own nodes, then the 128 slots from the partition before it, then the 128 from the one after. `send_rows`: local node indices within the sending partition. `send_count`: some list is full.
All inputs are finite; a program needn't handle non-finite values.
Results may differ from the reference program's by a relative error of at most 0.0046.
Values may be sent and summed in bfloat16 or wider, within the bound.
A program may use at most 32 MiB of HBM per device.

```python
import math
import jax
import jax.numpy as jnp
from jax import lax

D = 512
H = 512
SLOTS = 16
HALO = 128
NODES_DEV = 1024
NODES = 24576
LISTS = 48
N_DOM = 24


def draw_send_count(key, part):
    key = jax.random.fold_in(key, 11)
    counts = jax.random.randint(key, (LISTS,), HALO // 4, HALO + 1, dtype=jnp.int32)
    return counts.at[0].set(HALO)


def set_ends(array, key, smallest, high):
    extent = array.shape
    index_at = [jax.random.randint(jax.random.fold_in(key, axis), (), 0, extent[axis]) for axis in range(len(extent))]
    array = array.at[tuple(index_at)].set(smallest)
    longest = extent.index(max(extent))
    index_at[longest] = (index_at[longest] + 1) % extent[longest]
    return array.at[tuple(index_at)].set(high)


def block_scale(own_key, shape, pieces, smallest, largest):
    def one(position, parts):
        steps = jax.random.uniform(jax.random.fold_in(jax.random.fold_in(own_key, 6), position), (parts,), jnp.float32, smallest / len(pieces), largest / len(pieces))
        return jnp.repeat(jnp.exp(steps), shape[position] // parts).reshape((-1,) + (1,) * (len(shape) - position - 1))

    gain = one(*pieces[0])
    for cut in pieces[1:]:
        gain = gain * one(*cut)
    return gain


def centred(rng, extent, spread, reach, pieces=(), held_as=jnp.bfloat16):
    result = jax.random.normal(rng, extent, jnp.float32) * spread
    if len(pieces) > 0:
        result = block_scale(rng, extent, pieces, -0.22, 0.18) * result
    return jnp.clip(result, min=-reach, max=reach).astype(held_as)


def setup_inputs(seed: int = 0) -> dict:
    splits = jax.random.split(jax.random.key(seed), 9)
    return {
        "features": centred(splits[0], (D, NODES), 1.0, 6.0, ((0, 32), (1, 24))),
        "self_weight": centred(splits[1], (D, H), D ** -0.5, 0.25, ((1, 32),)),
        "neigh_weight": centred(splits[2], (D, H), D ** -0.5, 0.25, ((1, 32),)),
        "cotangent": centred(splits[3], (H, NODES), 1.0, 6.0, ((0, 32), (1, 24))),
        "neighbours": set_ends(jax.random.randint(splits[4], (NODES, SLOTS), 0, NODES_DEV + 2 * HALO), jax.random.fold_in(splits[4], 1), 0, (NODES_DEV + 2 * HALO) - 1).astype(jnp.int32),
        "degrees": set_ends(jax.random.randint(splits[5], (NODES,), 1, SLOTS + 1), jax.random.fold_in(splits[5], 1), 1, SLOTS).astype(jnp.int32),
        "send_rows": set_ends(jax.random.randint(splits[6], (LISTS, HALO), 0, NODES_DEV), jax.random.fold_in(splits[6], 1), 0, NODES_DEV - 1).astype(jnp.int32),
        "send_count": draw_send_count(jax.random.fold_in(splits[8], 71), 0),
    }


def edge_weights(degrees, slots):
    counted = jnp.arange(slots, dtype=jnp.int32)[:, None] < degrees[None, :]
    return jnp.where(counted, 1.0, 0.0).astype(jnp.float32) / degrees[None, :].astype(jnp.float32)

def gather_sum(extended, neighbour_t, weights):
    picked = extended[:, neighbour_t].astype(jnp.float32)
    return lax.optimization_barrier(jnp.sum(picked * weights[None], axis=1))

def spread_sum(grad_block, neighbour_t, weights, total_width):
    zeros_grid = jnp.zeros((grad_block.shape[0], total_width), jnp.float32)
    return zeros_grid.at[:, neighbour_t].add(grad_block[:, None, :] * weights[None])

def reference(features, self_weight, neigh_weight, cotangent, neighbours, degrees, send_rows, send_count):
    partitions = N_DOM
    in_width = features.shape[0]
    total_width = NODES_DEV + 2 * HALO
    blocks = features.reshape(in_width, partitions, NODES_DEV)
    list_rows = send_rows.reshape(partitions, 2, HALO)
    list_counts = send_count.reshape(partitions, 2)
    alive_mask = jnp.arange(HALO, dtype=jnp.int32)[None, None, :] < list_counts[:, :, None]
    picked = jax.vmap(lambda slab_x, list_idx: slab_x[:, list_idx], in_axes=(1, 0), out_axes=1)(blocks, list_rows)
    picked = jnp.where(alive_mask[None], picked, jnp.zeros((), features.dtype))
    from_left = jnp.roll(picked[:, :, 1], 1, axis=1)
    from_right = jnp.roll(picked[:, :, 0], -1, axis=1)
    extended = jnp.concatenate([blocks, from_left, from_right], axis=2).transpose(1, 0, 2)
    neighbour_t = neighbours.reshape(partitions, NODES_DEV, SLOTS).transpose(0, 2, 1)
    part_degrees = degrees.reshape(partitions, NODES_DEV)

    def forward_part(packed):
        weights = edge_weights(packed[2], SLOTS)
        return gather_sum(packed[0], packed[1], weights).astype(jnp.bfloat16)
    aggregate_rows = lax.map(forward_part, (extended, neighbour_t, part_degrees))
    aggregate_rows = aggregate_rows.transpose(1, 0, 2).reshape(in_width, partitions * NODES_DEV)
    preact = jnp.dot(self_weight.T, features, preferred_element_type=jnp.float32) + jnp.dot(neigh_weight.T, aggregate_rows, preferred_element_type=jnp.float32)
    activated = jax.nn.silu(preact).astype(jnp.bfloat16)
    sigmoid_z = jax.nn.sigmoid(preact)
    pre_grad = (cotangent.astype(jnp.float32) * sigmoid_z * (1.0 + preact * (1.0 - sigmoid_z))).astype(jnp.bfloat16)
    factor = 1.0 / math.sqrt(partitions * NODES_DEV)
    grad_self = jnp.dot(features, pre_grad.T, preferred_element_type=jnp.float32) * factor
    grad_neigh = jnp.dot(aggregate_rows, pre_grad.T, preferred_element_type=jnp.float32) * factor
    direct_grad = jnp.dot(self_weight, pre_grad, preferred_element_type=jnp.float32)
    agg_grad = jnp.dot(neigh_weight, pre_grad, preferred_element_type=jnp.float32)
    agg_parts = agg_grad.reshape(in_width, partitions, NODES_DEV).transpose(1, 0, 2)

    def backward_part(packed):
        weights = edge_weights(packed[2], SLOTS)
        return spread_sum(packed[0], packed[1], weights, total_width)
    ext_grad = lax.map(backward_part, (agg_parts, neighbour_t, part_degrees))
    local_grad = ext_grad[:, :, :NODES_DEV]
    left_grad = ext_grad[:, :, NODES_DEV:NODES_DEV + HALO]
    right_grad = ext_grad[:, :, NODES_DEV + HALO:]
    back_zero = jnp.roll(right_grad, 1, axis=0)
    back_one = jnp.roll(left_grad, -1, axis=0)
    returned = jnp.stack([back_zero, back_one], axis=1)
    returned = jnp.where(alive_mask[:, :, None, :], returned, 0.0)

    def add_back(grad_block, list_idx, back_block):
        flat_back = back_block.transpose(1, 0, 2).reshape(in_width, 2 * HALO)
        return grad_block.at[:, list_idx.reshape(-1)].add(flat_back)
    local_grad = jax.vmap(add_back)(local_grad, list_rows, returned)
    direct_parts = direct_grad.reshape(in_width, partitions, NODES_DEV).transpose(1, 0, 2)
    grad_x = (direct_parts + local_grad).transpose(1, 0, 2).reshape(in_width, partitions * NODES_DEV)
    return (activated, grad_x, grad_self, grad_neigh)
```

```python
import functools
import math

import jax
import jax.numpy as jnp
from jax import lax
from jax.experimental import pallas as pl
from jax.experimental.pallas import tpu as pltpu
from jax.sharding import PartitionSpec as P

MESH = pl.DeviceIdType.MESH
BF16 = jnp.bfloat16
F32 = jnp.float32

HALO, XS, WS, COT, AGG, ACT, PART, GRAD, BACK, RS, AG, N_SEMS = range(12)


def dot(a, b):
    return jnp.dot(a, b, preferred_element_type=F32)


def dot_t(a, b):
    return lax.dot_general(a, b, (((1,), (1,)), ((), ())), preferred_element_type=F32)


def split_dot_t(a, b):
    high = a.astype(BF16)
    low = (a - high.astype(F32)).astype(BF16)
    both = dot_t(jnp.concatenate([high, low], axis=0), b)
    return both[: a.shape[0]] + both[a.shape[0] :]


def layer_kernel(
    sizes,
    x_ref, w1_ref, w2_ref, cot_ref, nb_ref, deg_ref, rows_ref, count_ref,
    act_ref, gx_ref, gs_ref, gn_ref,
    chosen, edges, ids, live,
    halo_out, halo_in, x_out, x_in, w_out, w_in, cot_out, cot_in, agg_out, agg_in,
    act_out, act_in, part_out, part_in, grad_out, grad_in, back_out, back_in,
    rs_out, rs_in, ag_in,
    send_sem, recv_sem,
):
    n_dom, n_y, n_x, width, block, halo, slots, eb = sizes
    n_feat = n_y * n_x
    nodes = n_y * block
    n_pieces = rs_out.shape[0]
    piece_w = rs_out.shape[2]
    lane_pieces = w1_ref.shape[1] // piece_w
    me_d = lax.axis_index("dom")
    me_f = lax.axis_index("feat")
    me_y = me_f // n_x
    me_x = me_f % n_x

    def remote(src, dst, which, dom, feat):
        return pltpu.make_async_remote_copy(
            src_ref=src, dst_ref=dst, send_sem=send_sem.at[which], recv_sem=recv_sem.at[which],
            device_id={"dom": dom, "feat": feat}, device_id_type=MESH,
        )

    def arrived(ref, which):
        remote(ref, ref, which, me_d, me_f).wait_recv()

    def sent(ref, which):
        remote(ref, ref, which, me_d, me_f).wait_send()

    def each(count, body):
        def step(i, carry):
            body(i)
            return carry
        lax.fori_loop(0, count, step, 0)

    def to_feat(body):
        def one(i):
            other = lax.rem(me_f + 1 + i, n_feat)
            body(other, other // n_x)
        each(n_feat - 1, one)

    def to_y(body):
        def one(i):
            other = lax.rem(me_y + 1 + i, n_y)
            body(other * n_x + me_x, other)
        each(n_y - 1, one)

    barrier = pltpu.get_barrier_semaphore()

    def greet_feat(other, _):
        pl.semaphore_signal(barrier, inc=1, device_id={"dom": me_d, "feat": other}, device_id_type=MESH)

    def greet_dom(i):
        other = lax.rem(me_d + 1 + i, n_dom)
        pl.semaphore_signal(barrier, inc=1, device_id={"dom": other, "feat": me_f}, device_id_type=MESH)

    to_feat(greet_feat)
    each(n_dom - 1, greet_dom)

    slot_id = lax.broadcasted_iota(jnp.int32, (1, 2 * halo), 1)
    limit = jnp.where(slot_id < halo, count_ref[0], count_ref[1] + halo)
    rows = jnp.concatenate([rows_ref[0:1, :], rows_ref[1:2, :]], axis=1)
    rows = jnp.where(slot_id < limit, rows, -1)
    node_id = lax.broadcasted_iota(jnp.int32, (nodes, 2 * halo), 0)
    chosen[...] = jnp.where(node_id == rows, 1.0, 0.0).astype(BF16)
    x = x_ref[...]
    picked = dot(x, chosen[...]).astype(BF16)
    halo_out[0] = picked[:, :halo]
    halo_out[1] = picked[:, halo:]
    for y in range(n_y):
        x_out[y] = x[:, y * block : (y + 1) * block]
        cot_out[y] = cot_ref[:, y * block : (y + 1) * block]
    w_out[0] = w1_ref[...]
    w_out[1] = w2_ref[...]
    x_in[me_f] = x_out[me_y]
    cot_in[me_y] = cot_out[me_y]
    w_in[me_y] = w_out[...]

    pl.semaphore_wait(barrier, n_feat - 1 + n_dom - 1)

    before = lax.rem(me_d + n_dom - 1, n_dom)
    after = lax.rem(me_d + 1, n_dom)
    remote(halo_out.at[0], halo_in.at[1], HALO, before, me_f).start()
    remote(halo_out.at[1], halo_in.at[0], HALO, after, me_f).start()
    to_feat(lambda f, y: remote(x_out.at[y], x_in.at[me_f], XS, me_d, f).start())
    to_y(lambda f, y: remote(w_out, w_in.at[me_y], WS, me_d, f).start())
    to_y(lambda f, y: remote(cot_out.at[y], cot_in.at[me_y], COT, me_d, f).start())

    degree = deg_ref[...]
    slot = lax.broadcasted_iota(jnp.int32, (slots, nodes), 0)
    live[...] = jnp.where(slot < degree, nb_ref[...], -1)
    ids[...] = lax.broadcasted_iota(jnp.int32, (eb, block), 0).astype(F32).astype(BF16)
    inverse = 1.0 / degree.astype(F32)

    def count_edges(t):
        lanes = pl.ds(pl.multiple_of((t % n_y) * block, block), block)
        base = (t // n_y) * eb
        mine = (live[:, lanes] - base).astype(F32).astype(BF16)
        known = ids[...]
        total = jnp.zeros((eb, block), BF16)
        for k in range(slots):
            total = total + jnp.where(known == mine[k : k + 1, :], jnp.ones((), BF16), jnp.zeros((), BF16))
        edges[pl.ds(pl.multiple_of(base, eb), eb), lanes] = total

    each((nodes + 2 * halo) // eb * n_y, count_edges)

    mean = dot(x, edges[:nodes, :])
    arrived(halo_in, HALO)
    mean += dot(halo_in[0], edges[nodes : nodes + halo, :])
    mean += dot(halo_in[1], edges[nodes + halo :, :])
    mean = (mean * inverse).astype(BF16)
    for y in range(n_y):
        agg_out[y] = mean[:, y * block : (y + 1) * block]
    to_feat(lambda f, y: remote(agg_out.at[y], agg_in.at[me_f], AGG, me_d, f).start())
    agg_in[me_f] = agg_out[me_y]

    wide = w1_ref.shape[1]
    quarter = n_y * width
    arrived(w_in.at[pl.ds(0, n_y - 1)], WS)
    arrived(x_in.at[pl.ds(0, n_feat - 1)], XS)
    w1 = w_in[:, 0].reshape(quarter, wide)
    w2 = w_in[:, 1].reshape(quarter, wide)
    full_x = x_in[...].reshape(wide, block)
    preact = dot(w1, full_x)
    w1_t = w1.T
    w2_t = w2.T
    arrived(cot_in.at[pl.ds(0, n_y - 1)], COT)
    cot = cot_in[...].reshape(quarter, block).astype(F32)
    arrived(agg_in.at[pl.ds(0, n_feat - 1)], AGG)
    full_agg = agg_in[...].reshape(wide, block)
    preact += dot(w2, full_agg)
    s = jax.nn.sigmoid(preact)
    grad = (cot * s * (1.0 + preact * (1.0 - s))).astype(BF16)
    part_out[:, 0] = dot(w1_t, grad).astype(BF16).reshape(n_feat, width, block)
    part_out[:, 1] = dot(w2_t, grad).astype(BF16).reshape(n_feat, width, block)
    to_feat(lambda f, y: remote(part_out.at[f], part_in.at[me_f], PART, me_d, f).start())
    part_in[me_f] = part_out[me_f]

    grad_out[:, 0] = dot_t(grad, full_x).reshape(n_y, width, wide)
    grad_out[:, 1] = dot_t(grad, full_agg).reshape(n_y, width, wide)
    to_y(lambda f, y: remote(grad_out.at[y], grad_in.at[me_y], GRAD, me_d, f).start())
    grad_in[me_y] = grad_out[me_y]

    act_out[...] = (preact * s).astype(BF16).reshape(n_y, width, block)
    to_y(lambda f, y: remote(act_out.at[y], act_in.at[me_y], ACT, me_d, f).start())
    act_in[me_y] = act_out[me_y]

    arrived(part_in.at[pl.ds(0, n_feat - 1)], PART)
    direct, spread = [], []
    for y in range(n_y):
        here = part_in[pl.ds(y * n_x, n_x)].astype(F32)
        here = jnp.sum(here, axis=0)
        direct.append(here[0])
        spread.append(here[1])
    direct = jnp.concatenate(direct, axis=1)
    spread = jnp.concatenate(spread, axis=1) * inverse
    ext = split_dot_t(spread, edges[nodes:, :])
    back_out[0] = ext[:, :halo]
    back_out[1] = ext[:, halo:]
    remote(back_out.at[0], back_in.at[1], BACK, before, me_f).start()
    remote(back_out.at[1], back_in.at[0], BACK, after, me_f).start()

    arrived(grad_in.at[pl.ds(0, n_y - 1)], GRAD)
    weight_grad = jnp.sum(grad_in[...], axis=0)
    for piece in range(n_pieces):
        row, lane = piece // lane_pieces, piece % lane_pieces
        which, row = row // (width // 8), row % (width // 8)
        rs_out[piece] = weight_grad[which, row * 8 : (row + 1) * 8, lane * piece_w : (lane + 1) * piece_w]

    def scatter(i):
        other = lax.rem(me_d + 1 + i, n_dom)

        @pl.when(other < n_pieces)
        def _():
            remote(rs_out.at[other], rs_in.at[me_d], RS, other, me_f).start()

    each(n_dom - 1, scatter)

    gx = direct + split_dot_t(spread, edges[:nodes, :])

    @pl.when(me_d < n_pieces)
    def _():
        rs_in[me_d] = rs_out[me_d]
        arrived(rs_in.at[pl.ds(0, n_dom - 1)], RS)
        ag_in[me_d] = jnp.sum(rs_in[...], axis=0) * (1.0 / math.sqrt(nodes * n_dom))

        def give(i):
            other = lax.rem(me_d + 1 + i, n_dom)
            remote(ag_in.at[me_d], ag_in.at[me_d], AG, other, me_f).start()

        each(n_dom - 1, give)

    arrived(back_in, BACK)
    gx += split_dot_t(jnp.concatenate([back_in[0], back_in[1]], axis=1), chosen[...])
    gx_ref[...] = gx

    arrived(act_in.at[pl.ds(0, n_y - 1)], ACT)
    for y in range(n_y):
        act_ref[:, y * block : (y + 1) * block] = act_in[y]

    sent(halo_out, HALO)
    sent(x_in.at[pl.ds(0, n_feat - 1)], XS)
    sent(w_in.at[pl.ds(0, n_y - 1)], WS)
    sent(cot_in.at[pl.ds(0, n_y - 1)], COT)
    sent(agg_in.at[pl.ds(0, n_feat - 1)], AGG)
    sent(part_in.at[pl.ds(0, n_feat - 1)], PART)
    sent(grad_in.at[pl.ds(0, n_y - 1)], GRAD)
    sent(act_in.at[pl.ds(0, n_y - 1)], ACT)
    sent(back_out, BACK)

    @pl.when(me_d < n_pieces)
    def _():
        sent(rs_out.at[pl.ds(0, n_pieces - 1)], RS)
        sent(rs_in.at[pl.ds(0, n_dom - 1)], AG)
        arrived(ag_in.at[pl.ds(0, n_pieces - 1)], AG)

    @pl.when(me_d >= n_pieces)
    def _():
        sent(rs_out, RS)
        arrived(ag_in, AG)

    for piece in range(n_pieces):
        row, lane = piece // lane_pieces, piece % lane_pieces
        which, row = row // (width // 8), row % (width // 8)
        ref = gs_ref if which == 0 else gn_ref
        ref[row * 8 : (row + 1) * 8, lane * piece_w : (lane + 1) * piece_w] = ag_in[piece]


def per_device(
    n_x, features, self_weight, neigh_weight, cotangent, neighbours, degrees, send_rows, send_count
):
    width, nodes = features.shape
    wide = self_weight.shape[0]
    slots = neighbours.shape[1]
    halo = send_rows.shape[1]
    n_dom = lax.axis_size("dom")
    n_feat = lax.axis_size("feat")
    n_y = n_feat // n_x
    block = nodes // n_y
    eb = min(256, 2 * halo)
    piece_w = min(128, wide)
    n_pieces = 2 * (width // 8) * (wide // piece_w)
    sizes = (n_dom, n_y, n_x, width, block, halo, slots, eb)
    vmem = pl.BlockSpec(memory_space=pltpu.VMEM)
    tile = lambda *lead: pltpu.VMEM((*lead, width, block), BF16)
    act, gx, gs, gn = pl.pallas_call(
        functools.partial(layer_kernel, sizes),
        out_shape=(
            jax.ShapeDtypeStruct((width, nodes), BF16),
            jax.ShapeDtypeStruct((width, nodes), F32),
            jax.ShapeDtypeStruct((width, wide), F32),
            jax.ShapeDtypeStruct((width, wide), F32),
        ),
        in_specs=[vmem] * 7 + [pl.BlockSpec(memory_space=pltpu.SMEM)],
        out_specs=(vmem,) * 4,
        scratch_shapes=[
            pltpu.VMEM((nodes, 2 * halo), BF16),
            pltpu.VMEM((nodes + 2 * halo, nodes), BF16),
            pltpu.VMEM((eb, block), BF16),
            pltpu.VMEM((slots, nodes), jnp.int32),
            pltpu.VMEM((2, width, halo), BF16),
            pltpu.VMEM((2, width, halo), BF16),
            tile(n_y), tile(n_feat),
            pltpu.VMEM((2, width, wide), BF16),
            pltpu.VMEM((n_y, 2, width, wide), BF16),
            tile(n_y), tile(n_y),
            tile(n_y), tile(n_feat),
            tile(n_y), tile(n_y),
            tile(n_feat, 2), tile(n_feat, 2),
            pltpu.VMEM((n_y, 2, width, wide), F32),
            pltpu.VMEM((n_y, 2, width, wide), F32),
            pltpu.VMEM((2, width, halo), F32),
            pltpu.VMEM((2, width, halo), F32),
            pltpu.VMEM((n_pieces, 8, piece_w), F32),
            pltpu.VMEM((n_dom, 8, piece_w), F32),
            pltpu.VMEM((n_pieces, 8, piece_w), F32),
            pltpu.SemaphoreType.DMA((N_SEMS,)),
            pltpu.SemaphoreType.DMA((N_SEMS,)),
        ],
        compiler_params=pltpu.CompilerParams(
            collective_id=0, has_side_effects=True, vmem_limit_bytes=32 * 1024 * 1024
        ),
    )(
        features, self_weight.T, neigh_weight.T, cotangent, neighbours.T, degrees.reshape(1, nodes),
        send_rows, send_count,
    )
    return act, gx, gs.T, gn.T


def solution(mesh):
    n_x = 4 if mesh.shape["feat"] % 4 == 0 and mesh.shape["feat"] > 4 else 2
    return jax.shard_map(
        functools.partial(per_device, n_x),
        mesh=mesh,
        in_specs=(
            P("feat", "dom"),
            P(None, "feat"),
            P(None, "feat"),
            P("feat", "dom"),
            P("dom", None),
            P("dom"),
            P("dom", None),
            P("dom"),
        ),
        out_specs=(P("feat", "dom"), P("feat", "dom"), P(None, "feat"), P(None, "feat")),
        check_vma=False,
    )
```

```python
import functools
import math

import jax
import jax.numpy as jnp
from jax import lax
from jax.experimental import pallas as pl
from jax.experimental.pallas import tpu as pltpu
from jax.sharding import PartitionSpec as P

MESH = pl.DeviceIdType.MESH
BF16 = jnp.bfloat16
F32 = jnp.float32

HALO, XS, WS, WMATE, COT, AGG, ACT, PART, PAIR, GRAD, BACK, ACROSS, LAST, N_SEMS = range(14)
IN_X, IN_W1, IN_W2, IN_COT, IN_NB, IN_DEG, IN_ROWS, N_IN = range(8)


def dot(a, b):
    return jnp.dot(a, b, preferred_element_type=F32)


def dot_t(a, b):
    return lax.dot_general(a, b, (((1,), (1,)), ((), ())), preferred_element_type=F32)


def split_dot_t(a, b):
    high = a.astype(BF16)
    low = (a - high.astype(F32)).astype(BF16)
    both = dot_t(jnp.concatenate([high, low], axis=0), b)
    return both[: a.shape[0]] + both[a.shape[0] :]


def layer_kernel(
    sizes,
    x_hbm, w1_hbm, w2_hbm, cot_hbm, nb_hbm, deg_hbm, rows_hbm, count_ref,
    act_ref, gx_ref, gs_ref, gn_ref,
    x_ref, w_ref, cot_ref, nb_ref, deg_ref, rows_ref,
    chosen, edges, ids, live,
    halo_out, halo_in, x_out, x_in, w_in, w_mate, cot_out, cot_in, agg_out, agg_in,
    act_out, act_in, part_out, part_in, pair_out, pair_in, grad_out, grad_in, back_out, back_in,
    across_out, across_in, sums,
    send_sem, recv_sem, in_sem,
):
    n_dom, n_y, n_x, width, block, halo, slots, eb = sizes
    n_feat = n_y * n_x
    n_z = n_dom // 2
    nodes = n_y * block
    wide = w1_hbm.shape[1]
    me_d = lax.axis_index("dom")
    me_f = lax.axis_index("feat")
    me_y = me_f // n_x
    me_x = me_f % n_x
    me_z = me_d // 2
    core = me_d % 2
    mate = me_d + 1 - 2 * core
    before = lax.rem(me_d + n_dom - 1, n_dom)
    after = lax.rem(me_d + 1, n_dom)
    far = jnp.where(core == 0, before, after)

    loads = {}
    for which, src, dst in (
        (IN_X, x_hbm, x_ref), (IN_ROWS, rows_hbm, rows_ref), (IN_W1, w1_hbm, w_ref.at[0]), (IN_W2, w2_hbm, w_ref.at[1]),
        (IN_COT, cot_hbm, cot_ref), (IN_NB, nb_hbm, nb_ref), (IN_DEG, deg_hbm, deg_ref),
    ):
        loads[which] = pltpu.make_async_copy(src, dst, in_sem.at[which])
        loads[which].start()

    def remote(src, dst, which, dom, feat):
        return pltpu.make_async_remote_copy(
            src_ref=src, dst_ref=dst, send_sem=send_sem.at[which], recv_sem=recv_sem.at[which],
            device_id={"dom": dom, "feat": feat}, device_id_type=MESH,
        )

    def arrived(ref, which):
        remote(ref, ref, which, me_d, me_f).wait_recv()

    def sent(ref, which):
        remote(ref, ref, which, me_d, me_f).wait_send()

    def each(count, body):
        def step(i, carry):
            body(i)
            return carry
        lax.fori_loop(0, count, step, 0)

    def to_feat(body):
        def one(i):
            other = lax.rem(me_f + 1 + i, n_feat)
            body(other, other // n_x)
        each(n_feat - 1, one)

    def to_y(body):
        def one(i):
            other = lax.rem(me_y + 1 + i, n_y)
            body(other * n_x + me_x, other)
        each(n_y - 1, one)

    barrier = pltpu.get_barrier_semaphore()

    def greet(dom, feat):
        pl.semaphore_signal(barrier, inc=1, device_id={"dom": dom, "feat": feat}, device_id_type=MESH)

    def to_z(body):
        def one(i):
            other = lax.rem(me_z + 1 + i, n_z)
            body(other * 2 + core, other)
        each(n_z - 1, one)

    greet(far, me_f)
    greet(mate, me_f)
    to_feat(lambda f, y: greet(me_d, f))
    to_z(lambda d, z: greet(d, me_f))

    slot_id = lax.broadcasted_iota(jnp.int32, (1, 2 * halo), 1)
    limit = jnp.where(slot_id < halo, count_ref[0], count_ref[1] + halo)
    loads[IN_ROWS].wait()
    rows = jnp.concatenate([rows_ref[0:1, :], rows_ref[1:2, :]], axis=1)
    rows = jnp.where(slot_id < limit, rows, -1)
    node_id = lax.broadcasted_iota(jnp.int32, (nodes, 2 * halo), 0)
    chosen[...] = jnp.where(node_id == rows, 1.0, 0.0).astype(BF16)
    loads[IN_X].wait()
    x = x_ref[...]
    picked = dot(x, chosen[...]).astype(BF16)
    halo_out[0] = picked[:, :halo]
    halo_out[1] = picked[:, halo:]
    loads[IN_COT].wait()
    for y in range(n_y):
        x_out[y] = x[:, y * block : (y + 1) * block]
        cot_out[y] = cot_ref[:, y * block : (y + 1) * block]
    x_in[me_f] = x_out[me_y]
    cot_in[me_y] = cot_out[me_y]
    loads[IN_W1].wait()
    loads[IN_W2].wait()
    w_in[me_y] = w_ref[core]

    pl.semaphore_wait(barrier, n_feat - 1 + n_z - 1 + 2)

    remote(halo_out.at[0], halo_in.at[1], HALO, before, me_f).start()
    remote(halo_out.at[1], halo_in.at[0], HALO, after, me_f).start()
    to_y(lambda f, y: remote(w_ref.at[core], w_in.at[me_y], WS, me_d, f).start())
    to_feat(lambda f, y: remote(x_out.at[y], x_in.at[me_f], XS, me_d, f).start())
    to_y(lambda f, y: remote(cot_out.at[y], cot_in.at[me_y], COT, me_d, f).start())

    loads[IN_DEG].wait()
    loads[IN_NB].wait()
    degree = deg_ref[...]
    slot = lax.broadcasted_iota(jnp.int32, (slots, nodes), 0)
    live[...] = jnp.where(slot < degree, nb_ref[...], -1)
    ids[...] = lax.broadcasted_iota(jnp.int32, (eb, block), 0).astype(F32).astype(BF16)
    inverse = 1.0 / degree.astype(F32)

    def count_edges(t):
        lanes = pl.ds(pl.multiple_of((t % n_y) * block, block), block)
        base = (t // n_y) * eb
        mine = (live[:, lanes] - base).astype(F32).astype(BF16)
        known = ids[...]
        total = jnp.zeros((eb, block), BF16)
        for k in range(slots):
            total = total + jnp.where(known == mine[k : k + 1, :], jnp.ones((), BF16), jnp.zeros((), BF16))
        edges[pl.ds(pl.multiple_of(base, eb), eb), lanes] = total

    each((nodes + 2 * halo) // eb * n_y, count_edges)

    mean = dot(x, edges[:nodes, :])
    arrived(halo_in, HALO)
    mean += dot(halo_in[0], edges[nodes : nodes + halo, :])
    mean += dot(halo_in[1], edges[nodes + halo :, :])
    mean = (mean * inverse).astype(BF16)
    for y in range(n_y):
        agg_out[y] = mean[:, y * block : (y + 1) * block]
    to_feat(lambda f, y: remote(agg_out.at[y], agg_in.at[me_f], AGG, me_d, f).start())
    agg_in[me_f] = agg_out[me_y]

    quarter = n_y * width
    arrived(w_in.at[pl.ds(0, n_y - 1)], WS)
    remote(w_in, w_mate, WMATE, mate, me_f).start()
    arrived(x_in.at[pl.ds(0, n_feat - 1)], XS)
    full_x = x_in[...].reshape(wide, block)
    arrived(w_mate, WMATE)
    own_w = w_in[...].reshape(quarter, wide)
    other_w = w_mate[...].reshape(quarter, wide)
    w1 = jnp.where(core == 0, own_w, other_w)
    w2 = jnp.where(core == 0, other_w, own_w)
    preact = dot(w1, full_x)
    w1_t = w1.T
    w2_t = w2.T
    arrived(cot_in.at[pl.ds(0, n_y - 1)], COT)
    cot = cot_in[...].reshape(quarter, block).astype(F32)
    arrived(agg_in.at[pl.ds(0, n_feat - 1)], AGG)
    full_agg = agg_in[...].reshape(wide, block)
    preact += dot(w2, full_agg)
    s = jax.nn.sigmoid(preact)
    grad = (cot * s * (1.0 + preact * (1.0 - s))).astype(BF16)
    pair_out[0] = dot_t(grad, full_x)
    pair_out[1] = dot_t(grad, full_agg)
    remote(pair_out.at[1 - core], pair_in, PAIR, mate, me_f).start()

    part_out[:, 0] = dot(w1_t, grad).astype(BF16).reshape(n_feat, width, block)
    part_out[:, 1] = dot(w2_t, grad).astype(BF16).reshape(n_feat, width, block)
    part_in[me_f] = part_out[me_f]

    arrived(pair_in, PAIR)
    grad_out[...] = (pair_out[core] + pair_in[...]).astype(BF16).reshape(n_y, width, wide)
    to_y(lambda f, y: remote(grad_out.at[y], grad_in.at[me_y], GRAD, me_d, f).start())
    grad_in[me_y] = grad_out[me_y]
    to_feat(lambda f, y: remote(part_out.at[f], part_in.at[me_f], PART, me_d, f).start())

    act_out[...] = (preact * s).astype(BF16).reshape(n_y, width, block)
    to_y(lambda f, y: remote(act_out.at[y], act_in.at[me_y], ACT, me_d, f).start())
    act_in[me_y] = act_out[me_y]

    arrived(grad_in.at[pl.ds(0, n_y - 1)], GRAD)
    across_out[...] = jnp.sum(grad_in[...].astype(F32), axis=0).astype(BF16)
    to_z(lambda d, z: remote(across_out, across_in.at[me_z], ACROSS, d, me_f).start())
    across_in[me_z] = across_out[...]

    arrived(part_in.at[pl.ds(0, n_feat - 1)], PART)
    direct, spread = [], []
    for y in range(n_y):
        here = part_in[pl.ds(y * n_x, n_x)].astype(F32)
        here = jnp.sum(here, axis=0)
        direct.append(here[0])
        spread.append(here[1])
    direct = jnp.concatenate(direct, axis=1)
    spread = jnp.concatenate(spread, axis=1) * inverse
    ext = split_dot_t(spread, edges[nodes:, :])
    back_out[0] = ext[:, :halo]
    back_out[1] = ext[:, halo:]
    remote(back_out.at[0], back_in.at[1], BACK, before, me_f).start()
    remote(back_out.at[1], back_in.at[0], BACK, after, me_f).start()

    gx = direct + split_dot_t(spread, edges[:nodes, :])

    arrived(back_in, BACK)
    gx += split_dot_t(jnp.concatenate([back_in[0], back_in[1]], axis=1), chosen[...])
    gx_ref[...] = gx

    arrived(act_in.at[pl.ds(0, n_y - 1)], ACT)
    for y in range(n_y):
        act_ref[:, y * block : (y + 1) * block] = act_in[y]

    arrived(across_in.at[pl.ds(0, n_z - 1)], ACROSS)
    sums[core] = jnp.sum(across_in[...].astype(F32), axis=0) * (1.0 / math.sqrt(nodes * n_dom))
    last = remote(sums.at[core], sums.at[core], LAST, mate, me_f)
    last.start()

    sent(halo_out, HALO)
    sent(w_in.at[pl.ds(0, n_y - 1)], WS)
    sent(w_in, WMATE)
    sent(x_in.at[pl.ds(0, n_feat - 1)], XS)
    sent(cot_in.at[pl.ds(0, n_y - 1)], COT)
    sent(agg_in.at[pl.ds(0, n_feat - 1)], AGG)
    sent(pair_in, PAIR)
    sent(part_in.at[pl.ds(0, n_feat - 1)], PART)
    sent(grad_in.at[pl.ds(0, n_y - 1)], GRAD)
    sent(act_in.at[pl.ds(0, n_y - 1)], ACT)
    sent(back_out, BACK)
    sent(across_in.at[pl.ds(0, n_z - 1)], ACROSS)
    last.wait()
    gs_ref[...] = sums[0]
    gn_ref[...] = sums[1]


def hand_over(*refs):
    for src, dst in zip(refs[:4], refs[4:]):
        dst[...] = src[...]


def per_device(
    n_x, features, self_weight, neigh_weight, cotangent, neighbours, degrees, send_rows, send_count
):
    width, nodes = features.shape
    wide = self_weight.shape[0]
    slots = neighbours.shape[1]
    halo = send_rows.shape[1]
    n_dom = lax.axis_size("dom")
    n_feat = lax.axis_size("feat")
    n_y = n_feat // n_x
    block = nodes // n_y
    eb = min(256, 2 * halo)
    sizes = (n_dom, n_y, n_x, width, block, halo, slots, eb)
    vmem = pl.BlockSpec(memory_space=pltpu.VMEM)
    tile = lambda *lead: pltpu.VMEM((*lead, width, block), BF16)
    act, gx, gs, gn = pl.pallas_call(
        functools.partial(layer_kernel, sizes),
        out_shape=(
            jax.ShapeDtypeStruct((width, nodes), BF16),
            jax.ShapeDtypeStruct((width, nodes), F32),
            jax.ShapeDtypeStruct((width, wide), F32),
            jax.ShapeDtypeStruct((width, wide), F32),
        ),
        in_specs=[pl.BlockSpec(memory_space=pltpu.HBM)] * 7 + [pl.BlockSpec(memory_space=pltpu.SMEM)],
        out_specs=(vmem,) * 4,
        scratch_shapes=[
            pltpu.VMEM((width, nodes), BF16),
            pltpu.VMEM((2, width, wide), BF16),
            pltpu.VMEM((width, nodes), BF16),
            pltpu.VMEM((slots, nodes), jnp.int32),
            pltpu.VMEM((1, nodes), jnp.int32),
            pltpu.VMEM((2, halo), jnp.int32),
            pltpu.VMEM((nodes, 2 * halo), BF16),
            pltpu.VMEM((nodes + 2 * halo, nodes), BF16),
            pltpu.VMEM((eb, block), BF16),
            pltpu.VMEM((slots, nodes), jnp.int32),
            pltpu.VMEM((2, width, halo), BF16),
            pltpu.VMEM((2, width, halo), BF16),
            tile(n_y), tile(n_feat),
            pltpu.VMEM((n_y, width, wide), BF16),
            pltpu.VMEM((n_y, width, wide), BF16),
            tile(n_y), tile(n_y),
            tile(n_y), tile(n_feat),
            tile(n_y), tile(n_y),
            tile(n_feat, 2), tile(n_feat, 2),
            pltpu.VMEM((2, n_y * width, wide), F32),
            pltpu.VMEM((n_y * width, wide), F32),
            pltpu.VMEM((n_y, width, wide), BF16),
            pltpu.VMEM((n_y, width, wide), BF16),
            pltpu.VMEM((2, width, halo), F32),
            pltpu.VMEM((2, width, halo), F32),
            pltpu.VMEM((width, wide), BF16),
            pltpu.VMEM((n_dom // 2, width, wide), BF16),
            pltpu.VMEM((2, width, wide), F32),
            pltpu.SemaphoreType.DMA((N_SEMS,)),
            pltpu.SemaphoreType.DMA((N_SEMS,)),
            pltpu.SemaphoreType.DMA((N_IN,)),
        ],
        compiler_params=pltpu.CompilerParams(
            collective_id=0, has_side_effects=True, vmem_limit_bytes=64 * 1024 * 1024
        ),
    )(
        features, self_weight.T, neigh_weight.T, cotangent, neighbours.T, degrees.reshape(1, nodes),
        send_rows, send_count,
    )
    act, gx, gs, gn = pl.pallas_call(
        hand_over,
        out_shape=tuple(jax.ShapeDtypeStruct(a.shape, a.dtype) for a in (act, gx, gs, gn)),
        in_specs=[vmem] * 4,
        out_specs=(vmem,) * 4,
    )(act, gx, gs, gn)
    return act, gx, gs.T, gn.T


def solution(mesh):
    n_x = 4 if mesh.shape["feat"] % 4 == 0 and mesh.shape["feat"] > 4 else 2
    return jax.shard_map(
        functools.partial(per_device, n_x),
        mesh=mesh,
        in_specs=(
            P("feat", "dom"),
            P(None, "feat"),
            P(None, "feat"),
            P("feat", "dom"),
            P("dom", None),
            P("dom"),
            P("dom", None),
            P("dom"),
        ),
        out_specs=(P("feat", "dom"), P("feat", "dom"), P(None, "feat"), P(None, "feat")),
        check_vma=False,
    )
```

```python
import functools
import math

import jax
import jax.numpy as jnp
from jax import lax
from jax.experimental import pallas as pl
from jax.experimental.pallas import tpu as pltpu
from jax.sharding import PartitionSpec as P

MESH = pl.DeviceIdType.MESH
BF16 = jnp.bfloat16
F32 = jnp.float32

HALO, XY, XX, WS, WMATE, COT, AGG, ACT, PART, PAIR, GRAD, BACK, ACROSS, LAST, N_SEMS = range(15)
IN_X, IN_W1, IN_W2, IN_COT, IN_NB, IN_DEG, IN_ROWS, N_IN = range(8)


def dot(a, b):
    return jnp.dot(a, b, preferred_element_type=F32)


def dot_t(a, b):
    return lax.dot_general(a, b, (((1,), (1,)), ((), ())), preferred_element_type=F32)


def split_dot_t(a, b):
    high = a.astype(BF16)
    low = (a - high.astype(F32)).astype(BF16)
    both = dot_t(jnp.concatenate([high, low], axis=0), b)
    return both[: a.shape[0]] + both[a.shape[0] :]


def layer_kernel(
    sizes,
    x_hbm, w1_hbm, w2_hbm, cot_hbm, nb_hbm, deg_hbm, rows_hbm, count_ref,
    act_ref, gx_ref, gs_ref, gn_ref,
    w_ref, cot_ref, nb_ref, deg_ref, rows_ref,
    ext, chosen, edges, ids, live, inverse_ref,
    halo_out, halo_in, x_out, x_y, x_in, w_in, w_mate, cot_out, cot_in, agg_out, agg_in,
    act_out, act_in, part_out, part_in, pair_out, pair_in, grad_out, grad_in, back_out, back_in,
    across_out, across_in, sums,
    send_sem, recv_sem, in_sem,
):
    n_dom, n_y, n_x, width, block, halo, slots, eb = sizes
    n_feat = n_y * n_x
    n_z = n_dom // 2
    nodes = n_y * block
    wide = w1_hbm.shape[1]
    me_d = lax.axis_index("dom")
    me_f = lax.axis_index("feat")
    me_y = me_f // n_x
    me_x = me_f % n_x
    me_z = me_d // 2
    core = me_d % 2
    mate = me_d + 1 - 2 * core
    before = lax.rem(me_d + n_dom - 1, n_dom)
    after = lax.rem(me_d + 1, n_dom)
    far = jnp.where(core == 0, before, after)

    loads = {}
    for which, src, dst in (
        (IN_X, x_hbm, ext.at[:, pl.ds(0, nodes)]), (IN_ROWS, rows_hbm, rows_ref), (IN_NB, nb_hbm, nb_ref),
        (IN_DEG, deg_hbm, deg_ref), (IN_W1, w1_hbm, w_ref.at[0]), (IN_W2, w2_hbm, w_ref.at[1]), (IN_COT, cot_hbm, cot_ref),
    ):
        loads[which] = pltpu.make_async_copy(src, dst, in_sem.at[which])
        loads[which].start()

    def remote(src, dst, which, dom, feat):
        return pltpu.make_async_remote_copy(
            src_ref=src, dst_ref=dst, send_sem=send_sem.at[which], recv_sem=recv_sem.at[which],
            device_id={"dom": dom, "feat": feat}, device_id_type=MESH,
        )

    def arrived(ref, which):
        remote(ref, ref, which, me_d, me_f).wait_recv()

    def sent(ref, which):
        remote(ref, ref, which, me_d, me_f).wait_send()

    def each(count, body):
        def step(i, carry):
            body(i)
            return carry
        lax.fori_loop(0, count, step, 0)

    def from_half(i, count):
        return 1 + lax.rem(i + max(3 * count // 8 - 1, 0), count - 1)

    def to_feat(body):
        def one(i):
            other = lax.rem(me_f + from_half(i, n_feat), n_feat)
            body(other, other // n_x)
        each(n_feat - 1, one)

    def to_y(body):
        def one(i):
            other = lax.rem(me_y + from_half(i, n_y), n_y)
            body(other * n_x + me_x, other)
        each(n_y - 1, one)

    def to_x(body):
        def one(i):
            other = lax.rem(me_x + 1 + i, n_x)
            body(me_y * n_x + other, other)
        each(n_x - 1, one)

    barrier = pltpu.get_barrier_semaphore()

    def greet(dom, feat):
        pl.semaphore_signal(barrier, inc=1, device_id={"dom": dom, "feat": feat}, device_id_type=MESH)

    def to_z(body):
        def one(i):
            other = lax.rem(me_z + from_half(i, n_z), n_z)
            body(other * 2 + core, other)
        each(n_z - 1, one)

    greet(far, me_f)
    greet(mate, me_f)
    to_feat(lambda f, y: greet(me_d, f))
    to_z(lambda d, z: greet(d, me_f))

    slot_id = lax.broadcasted_iota(jnp.int32, (1, 2 * halo), 1)
    limit = jnp.where(slot_id < halo, count_ref[0], count_ref[1] + halo)
    loads[IN_ROWS].wait()
    rows = jnp.concatenate([rows_ref[0:1, :], rows_ref[1:2, :]], axis=1)
    rows = jnp.where(slot_id < limit, rows, -1)
    node_id = lax.broadcasted_iota(jnp.int32, (nodes, 2 * halo), 0)
    chosen[...] = jnp.where(node_id == rows, 1.0, 0.0).astype(BF16)
    loads[IN_X].wait()
    x = ext[:, :nodes]
    picked = dot(x, chosen[...]).astype(BF16)
    halo_out[0] = picked[:, :halo]
    halo_out[1] = picked[:, halo:]
    for y in range(n_y):
        x_out[y] = x[:, y * block : (y + 1) * block]
    x_y[me_y] = x_out[me_y]

    loads[IN_DEG].wait()
    loads[IN_NB].wait()
    degree = deg_ref[...]
    slot = lax.broadcasted_iota(jnp.int32, (slots, nodes), 0)
    live[...] = jnp.where(slot < degree, nb_ref[...], -1)
    ids[...] = lax.broadcasted_iota(jnp.int32, (eb, 2 * block), 0).astype(F32).astype(BF16)
    inverse = 1.0 / degree.astype(F32)
    inverse_ref[...] = inverse

    n_pairs = n_y // 2
    pairs = [lax.rem(me_y // 2 + off, n_pairs) for off in sorted(range(n_pairs), key=lambda o: -min(o, n_pairs - o))]

    def pair_lanes(pair):
        return pl.ds(pl.multiple_of(pair * 2 * block, 2 * block), 2 * block)

    def count_edges(pair):
        lanes = pair_lanes(pair)

        def one(t):
            base = t * eb
            mine = (live[:, lanes] - base).astype(F32).astype(BF16)
            known = ids[...]
            total = jnp.zeros((eb, 2 * block), BF16)
            for k in range(slots):
                total = total + jnp.where(known == mine[k : k + 1, :], jnp.ones((), BF16), jnp.zeros((), BF16))
            edges[pl.ds(pl.multiple_of(base, eb), eb), lanes] = total

        each((nodes + 2 * halo) // eb, one)

    for pair in pairs[:-1]:
        count_edges(pair)

    loads[IN_COT].wait()
    for y in range(n_y):
        cot_out[y] = cot_ref[:, y * block : (y + 1) * block]
    cot_in[me_y] = cot_out[me_y]
    loads[IN_W1].wait()
    loads[IN_W2].wait()
    w_in[me_y] = w_ref[core]

    pl.semaphore_wait(barrier, n_feat - 1 + n_z - 1 + 2)

    remote(halo_out.at[0], halo_in.at[1], HALO, before, me_f).start()
    remote(halo_out.at[1], halo_in.at[0], HALO, after, me_f).start()
    to_y(lambda f, y: remote(x_out.at[y], x_y.at[me_y], XY, me_d, f).start())
    to_y(lambda f, y: remote(w_ref.at[core], w_in.at[me_y], WS, me_d, f).start())
    to_y(lambda f, y: remote(cot_out.at[y], cot_in.at[me_y], COT, me_d, f).start())

    count_edges(pairs[-1])
    arrived(halo_in, HALO)
    ext[:, nodes : nodes + halo] = halo_in[0]
    ext[:, nodes + halo :] = halo_in[1]
    for pair in pairs:
        lanes = pair_lanes(pair)
        mean = (dot(ext[...], edges[:, lanes]) * inverse_ref[:, lanes]).astype(BF16)
        agg_out[pair * 2] = mean[:, :block]
        agg_out[pair * 2 + 1] = mean[:, block:]

        def give(i):
            y = pair * 2 + i // n_x
            other = y * n_x + lax.rem(me_x + i, n_x)

            @pl.when(other != me_f)
            def _():
                remote(agg_out.at[y], agg_in.at[me_f], AGG, me_d, other).start()

        each(2 * n_x, give)
    agg_in[me_f] = agg_out[me_y]

    arrived(x_y.at[pl.ds(0, n_y - 1)], XY)
    to_x(lambda f, x: remote(x_y, x_in.at[:, me_x], XX, me_d, f).start())
    x_in[:, me_x] = x_y[...]

    quarter = n_y * width
    arrived(w_in.at[pl.ds(0, n_y - 1)], WS)
    remote(w_in, w_mate, WMATE, mate, me_f).start()
    arrived(x_in.at[:, pl.ds(0, n_x - 1)], XX)
    full_x = x_in[...].reshape(wide, block)
    arrived(w_mate, WMATE)
    own_w = w_in[...].reshape(quarter, wide)
    other_w = w_mate[...].reshape(quarter, wide)
    w1 = jnp.where(core == 0, own_w, other_w)
    w2 = jnp.where(core == 0, other_w, own_w)
    preact = dot(w1, full_x)
    w1_t = w1.T
    w2_t = w2.T
    arrived(cot_in.at[pl.ds(0, n_y - 1)], COT)
    cot = cot_in[...].reshape(quarter, block).astype(F32)
    arrived(agg_in.at[pl.ds(0, n_feat - 1)], AGG)
    full_agg = agg_in[...].reshape(wide, block)
    preact += dot(w2, full_agg)
    s = jax.nn.sigmoid(preact)
    grad = (cot * s * (1.0 + preact * (1.0 - s))).astype(BF16)
    pair_out[0] = dot_t(grad, full_x)
    pair_out[1] = dot_t(grad, full_agg)
    remote(pair_out.at[1 - core], pair_in, PAIR, mate, me_f).start()

    part_out[:, 0] = dot(w1_t, grad).astype(BF16).reshape(n_feat, width, block)
    part_out[:, 1] = dot(w2_t, grad).astype(BF16).reshape(n_feat, width, block)
    part_in[me_f] = part_out[me_f]

    arrived(pair_in, PAIR)
    grad_out[...] = (pair_out[core] + pair_in[...]).astype(BF16).reshape(n_y, width, wide)
    to_y(lambda f, y: remote(grad_out.at[y], grad_in.at[me_y], GRAD, me_d, f).start())
    grad_in[me_y] = grad_out[me_y]
    to_feat(lambda f, y: remote(part_out.at[f], part_in.at[me_f], PART, me_d, f).start())

    act_out[...] = (preact * s).astype(BF16).reshape(n_y, width, block)
    to_y(lambda f, y: remote(act_out.at[y], act_in.at[me_y], ACT, me_d, f).start())
    act_in[me_y] = act_out[me_y]

    arrived(grad_in.at[pl.ds(0, n_y - 1)], GRAD)
    across_out[...] = jnp.sum(grad_in[...].astype(F32), axis=0).astype(BF16)
    to_z(lambda d, z: remote(across_out, across_in.at[me_z], ACROSS, d, me_f).start())
    across_in[me_z] = across_out[...]

    arrived(part_in.at[pl.ds(0, n_feat - 1)], PART)
    direct, spread = [], []
    for y in range(n_y):
        here = part_in[pl.ds(y * n_x, n_x)].astype(F32)
        here = jnp.sum(here, axis=0)
        direct.append(here[0])
        spread.append(here[1])
    direct = jnp.concatenate(direct, axis=1)
    spread = jnp.concatenate(spread, axis=1) * inverse
    ext = split_dot_t(spread, edges[nodes:, :])
    back_out[0] = ext[:, :halo]
    back_out[1] = ext[:, halo:]
    remote(back_out.at[0], back_in.at[1], BACK, before, me_f).start()
    remote(back_out.at[1], back_in.at[0], BACK, after, me_f).start()

    gx = direct + split_dot_t(spread, edges[:nodes, :])

    arrived(back_in, BACK)
    gx += split_dot_t(jnp.concatenate([back_in[0], back_in[1]], axis=1), chosen[...])
    gx_ref[...] = gx

    arrived(act_in.at[pl.ds(0, n_y - 1)], ACT)
    for y in range(n_y):
        act_ref[:, y * block : (y + 1) * block] = act_in[y]

    arrived(across_in.at[pl.ds(0, n_z - 1)], ACROSS)
    sums[core] = jnp.sum(across_in[...].astype(F32), axis=0) * (1.0 / math.sqrt(nodes * n_dom))
    last = remote(sums.at[core], sums.at[core], LAST, mate, me_f)
    last.start()

    sent(halo_out, HALO)
    sent(w_in.at[pl.ds(0, n_y - 1)], WS)
    sent(w_in, WMATE)
    sent(x_y.at[pl.ds(0, n_y - 1)], XY)
    sent(x_in.at[:, pl.ds(0, n_x - 1)], XX)
    sent(cot_in.at[pl.ds(0, n_y - 1)], COT)
    sent(agg_in.at[pl.ds(0, n_feat - 1)], AGG)
    sent(pair_in, PAIR)
    sent(part_in.at[pl.ds(0, n_feat - 1)], PART)
    sent(grad_in.at[pl.ds(0, n_y - 1)], GRAD)
    sent(act_in.at[pl.ds(0, n_y - 1)], ACT)
    sent(back_out, BACK)
    sent(across_in.at[pl.ds(0, n_z - 1)], ACROSS)
    last.wait()
    gs_ref[...] = sums[0]
    gn_ref[...] = sums[1]


def hand_over(*refs):
    for src, dst in zip(refs[:4], refs[4:]):
        dst[...] = src[...]


def per_device(
    n_x, features, self_weight, neigh_weight, cotangent, neighbours, degrees, send_rows, send_count
):
    width, nodes = features.shape
    wide = self_weight.shape[0]
    slots = neighbours.shape[1]
    halo = send_rows.shape[1]
    n_dom = lax.axis_size("dom")
    n_feat = lax.axis_size("feat")
    n_y = n_feat // n_x
    block = nodes // n_y
    eb = min(256, 2 * halo)
    sizes = (n_dom, n_y, n_x, width, block, halo, slots, eb)
    vmem = pl.BlockSpec(memory_space=pltpu.VMEM)
    tile = lambda *lead: pltpu.VMEM((*lead, width, block), BF16)
    act, gx, gs, gn = pl.pallas_call(
        functools.partial(layer_kernel, sizes),
        out_shape=(
            jax.ShapeDtypeStruct((width, nodes), BF16),
            jax.ShapeDtypeStruct((width, nodes), F32),
            jax.ShapeDtypeStruct((width, wide), F32),
            jax.ShapeDtypeStruct((width, wide), F32),
        ),
        in_specs=[pl.BlockSpec(memory_space=pltpu.HBM)] * 7 + [pl.BlockSpec(memory_space=pltpu.SMEM)],
        out_specs=(vmem,) * 4,
        scratch_shapes=[
            pltpu.VMEM((2, width, wide), BF16),
            pltpu.VMEM((width, nodes), BF16),
            pltpu.VMEM((slots, nodes), jnp.int32),
            pltpu.VMEM((1, nodes), jnp.int32),
            pltpu.VMEM((2, halo), jnp.int32),
            pltpu.VMEM((width, nodes + 2 * halo), BF16),
            pltpu.VMEM((nodes, 2 * halo), BF16),
            pltpu.VMEM((nodes + 2 * halo, nodes), BF16),
            pltpu.VMEM((eb, 2 * block), BF16),
            pltpu.VMEM((slots, nodes), jnp.int32),
            pltpu.VMEM((1, nodes), F32),
            pltpu.VMEM((2, width, halo), BF16),
            pltpu.VMEM((2, width, halo), BF16),
            tile(n_y), tile(n_y), tile(n_y, n_x),
            pltpu.VMEM((n_y, width, wide), BF16),
            pltpu.VMEM((n_y, width, wide), BF16),
            tile(n_y), tile(n_y),
            tile(n_y), tile(n_feat),
            tile(n_y), tile(n_y),
            tile(n_feat, 2), tile(n_feat, 2),
            pltpu.VMEM((2, n_y * width, wide), F32),
            pltpu.VMEM((n_y * width, wide), F32),
            pltpu.VMEM((n_y, width, wide), BF16),
            pltpu.VMEM((n_y, width, wide), BF16),
            pltpu.VMEM((2, width, halo), F32),
            pltpu.VMEM((2, width, halo), F32),
            pltpu.VMEM((width, wide), BF16),
            pltpu.VMEM((n_dom // 2, width, wide), BF16),
            pltpu.VMEM((2, width, wide), F32),
            pltpu.SemaphoreType.DMA((N_SEMS,)),
            pltpu.SemaphoreType.DMA((N_SEMS,)),
            pltpu.SemaphoreType.DMA((N_IN,)),
        ],
        compiler_params=pltpu.CompilerParams(
            collective_id=0, has_side_effects=True, vmem_limit_bytes=64 * 1024 * 1024
        ),
    )(
        features, self_weight.T, neigh_weight.T, cotangent, neighbours.T, degrees.reshape(1, nodes),
        send_rows, send_count,
    )
    act, gx, gs, gn = pl.pallas_call(
        hand_over,
        out_shape=tuple(jax.ShapeDtypeStruct(a.shape, a.dtype) for a in (act, gx, gs, gn)),
        in_specs=[vmem] * 4,
        out_specs=(vmem,) * 4,
    )(act, gx, gs, gn)
    return act, gx, gs.T, gn.T


def solution(mesh):
    n_x = 4 if mesh.shape["feat"] % 4 == 0 and mesh.shape["feat"] > 4 else 2
    return jax.shard_map(
        functools.partial(per_device, n_x),
        mesh=mesh,
        in_specs=(
            P("feat", "dom"),
            P(None, "feat"),
            P(None, "feat"),
            P("feat", "dom"),
            P("dom", None),
            P("dom"),
            P("dom", None),
            P("dom"),
        ),
        out_specs=(P("feat", "dom"), P("feat", "dom"), P(None, "feat"), P(None, "feat")),
        check_vma=False,
    )
```

```python
import functools
import math

import jax
import jax.numpy as jnp
from jax import lax
from jax.experimental import pallas as pl
from jax.experimental.pallas import tpu as pltpu
from jax.sharding import PartitionSpec as P

MESH = pl.DeviceIdType.MESH
BF16 = jnp.bfloat16
F32 = jnp.float32

HALO, XY, XX, WS, WMATE, COT, AGG, ACT, DIRECT, SPREAD, PAIR, BACK, LAST, GRAD, GRAD_2, ACROSS, ACROSS_2, N_SEMS = range(18)
IN_X, IN_W1, IN_W2, IN_COT, IN_NB, IN_DEG, IN_ROWS, N_IN = range(8)


def dot(a, b):
    return jnp.dot(a, b, preferred_element_type=F32)


def dot_t(a, b):
    return lax.dot_general(a, b, (((1,), (1,)), ((), ())), preferred_element_type=F32)


def split_dot_t(a, b):
    high = a.astype(BF16)
    low = (a - high.astype(F32)).astype(BF16)
    both = dot_t(jnp.concatenate([high, low], axis=0), b)
    return both[: a.shape[0]] + both[a.shape[0] :]


def layer_kernel(
    sizes,
    x_hbm, w1_hbm, w2_hbm, cot_hbm, nb_hbm, deg_hbm, rows_hbm, count_ref,
    act_ref, gx_ref, gs_ref, gn_ref,
    w_ref, cot_ref, nb_ref, deg_ref, rows_ref,
    ext, chosen, edges, low_ref, unit_ref, inverse_ref,
    halo_out, halo_in, x_out, x_y, x_in, w_in, w_mate, cot_out, cot_in, agg_out, agg_in,
    act_out, act_in, part_out, part_in, pair_out, pair_in, grad_out, grad_in, back_out, back_in,
    across_out, across_in, sums,
    send_sem, recv_sem, in_sem,
):
    n_dom, n_y, n_x, width, block, halo, slots, eb = sizes
    n_feat = n_y * n_x
    n_z = n_dom // 2
    nodes = n_y * block
    wide = w1_hbm.shape[1]
    half_wide = wide // 2
    me_d = lax.axis_index("dom")
    me_f = lax.axis_index("feat")
    me_y = me_f // n_x
    me_x = me_f % n_x
    me_z = me_d // 2
    core = me_d % 2
    mate = me_d + 1 - 2 * core
    before = lax.rem(me_d + n_dom - 1, n_dom)
    after = lax.rem(me_d + 1, n_dom)
    far = jnp.where(core == 0, before, after)

    loads = {}
    for which, src, dst in (
        (IN_X, x_hbm, ext.at[:, pl.ds(0, nodes)]), (IN_ROWS, rows_hbm, rows_ref), (IN_NB, nb_hbm, nb_ref),
        (IN_DEG, deg_hbm, deg_ref), (IN_W1, w1_hbm, w_ref.at[0]), (IN_W2, w2_hbm, w_ref.at[1]), (IN_COT, cot_hbm, cot_ref),
    ):
        loads[which] = pltpu.make_async_copy(src, dst, in_sem.at[which])
        loads[which].start()

    def remote(src, dst, which, dom, feat):
        return pltpu.make_async_remote_copy(
            src_ref=src, dst_ref=dst, send_sem=send_sem.at[which], recv_sem=recv_sem.at[which],
            device_id={"dom": dom, "feat": feat}, device_id_type=MESH,
        )

    def arrived(ref, which):
        remote(ref, ref, which, me_d, me_f).wait_recv()

    def sent(ref, which):
        remote(ref, ref, which, me_d, me_f).wait_send()

    def each(count, body):
        def step(i, carry):
            body(i)
            return carry
        lax.fori_loop(0, count, step, 0)

    def from_half(i, count):
        return 1 + lax.rem(i + max(3 * count // 8 - 1, 0), count - 1)

    def to_feat(body):
        def one(i):
            other = lax.rem(me_f + from_half(i, n_feat), n_feat)
            body(other, other // n_x)
        each(n_feat - 1, one)

    def to_y(body):
        def one(i):
            other = lax.rem(me_y + from_half(i, n_y), n_y)
            body(other * n_x + me_x, other)
        each(n_y - 1, one)

    def to_x(body):
        def one(i):
            other = lax.rem(me_x + 1 + i, n_x)
            body(me_y * n_x + other, other)
        each(n_x - 1, one)

    barrier = pltpu.get_barrier_semaphore()

    def greet(dom, feat):
        pl.semaphore_signal(barrier, inc=1, device_id={"dom": dom, "feat": feat}, device_id_type=MESH)

    def to_z(body):
        def one(i):
            other = lax.rem(me_z + from_half(i, n_z), n_z)
            body(other * 2 + core, other)
        each(n_z - 1, one)

    greet(far, me_f)
    to_z(lambda d, z: greet(d, me_f))
    to_feat(lambda f, y: greet(me_d, f))
    greet(mate, me_f)

    slot_id = lax.broadcasted_iota(jnp.int32, (1, 2 * halo), 1)
    limit = jnp.where(slot_id < halo, count_ref[0], count_ref[1] + halo)
    loads[IN_ROWS].wait()
    rows = jnp.concatenate([rows_ref[0:1, :], rows_ref[1:2, :]], axis=1)
    rows = jnp.where(slot_id < limit, rows, -1)
    node_id = lax.broadcasted_iota(jnp.int32, (nodes, 2 * halo), 0)
    chosen[...] = jnp.where(node_id == rows, 1.0, 0.0).astype(BF16)
    loads[IN_X].wait()
    x = ext[:, :nodes]
    picked = dot(x, chosen[...]).astype(BF16)
    halo_out[0] = picked[:, :halo]
    halo_out[1] = picked[:, halo:]
    for y in range(n_y):
        x_out[y] = x[:, y * block : (y + 1) * block]
    x_y[me_y] = x_out[me_y]

    loads[IN_DEG].wait()
    loads[IN_NB].wait()
    degree = deg_ref[...]
    slot = lax.broadcasted_iota(jnp.int32, (slots, nodes), 0)
    nb = nb_ref[...]
    low_ref[...] = jnp.where(slot < degree, nb % eb, -1)
    unit_ref[...] = jnp.left_shift(jnp.ones_like(nb), 6 * (nb // eb))
    inverse = 1.0 / degree.astype(F32)
    inverse_ref[...] = inverse

    n_pairs = n_y // 2
    pairs = [lax.rem(me_y // 2 + off, n_pairs) for off in sorted(range(n_pairs), key=lambda o: -min(o, n_pairs - o))]

    def pair_lanes(pair):
        return pl.ds(pl.multiple_of(pair * 2 * block, 2 * block), 2 * block)

    def count_edges(pair):
        rows_once = min(128, eb)

        def one(t):
            lanes = pl.ds(pl.multiple_of((pair * 2 + t % 2) * block, block), block)
            base = (t // 2) * rows_once
            low = low_ref[:, lanes] - base
            unit = unit_ref[:, lanes]
            known = lax.broadcasted_iota(jnp.int32, (rows_once, block), 0)
            total = jnp.zeros((rows_once, block), jnp.int32)
            for k in range(slots):
                total = total + jnp.where(known == low[k : k + 1, :], unit[k : k + 1, :], 0)
            for high in range((nodes + 2 * halo) // eb):
                count = ((total >> (6 * high)) & 63).astype(F32).astype(BF16)
                edges[pl.ds(pl.multiple_of(high * eb + base, rows_once), rows_once), lanes] = count

        each(2 * eb // rows_once, one)

    for pair in pairs[:2]:
        count_edges(pair)

    loads[IN_COT].wait()
    for y in range(n_y):
        cot_out[y] = cot_ref[:, y * block : (y + 1) * block]
    cot_in[me_y] = cot_out[me_y]
    loads[IN_W1].wait()
    loads[IN_W2].wait()
    w_in[me_y] = w_ref[core]

    pl.semaphore_wait(barrier, n_feat - 1 + n_z - 1 + 2)

    remote(halo_out.at[0], halo_in.at[1], HALO, before, me_f).start()
    remote(halo_out.at[1], halo_in.at[0], HALO, after, me_f).start()
    to_y(lambda f, y: remote(x_out.at[y], x_y.at[me_y], XY, me_d, f).start())
    to_y(lambda f, y: remote(w_ref.at[core], w_in.at[me_y], WS, me_d, f).start())
    to_y(lambda f, y: remote(cot_out.at[y], cot_in.at[me_y], COT, me_d, f).start())

    for pair in pairs[2:]:
        count_edges(pair)
    arrived(halo_in, HALO)
    ext[:, nodes : nodes + halo] = halo_in[0]
    ext[:, nodes + halo :] = halo_in[1]
    for pair in pairs:
        lanes = pair_lanes(pair)
        mean = (dot(ext[...], edges[:, lanes]) * inverse_ref[:, lanes]).astype(BF16)
        agg_out[pair * 2] = mean[:, :block]
        agg_out[pair * 2 + 1] = mean[:, block:]

        def give(i):
            y = pair * 2 + i // n_x
            other = y * n_x + lax.rem(me_x + i, n_x)

            @pl.when(other != me_f)
            def _():
                remote(agg_out.at[y], agg_in.at[me_f], AGG, me_d, other).start()

        each(2 * n_x, give)
    agg_in[me_f] = agg_out[me_y]

    arrived(x_y.at[pl.ds(0, n_y - 1)], XY)
    to_x(lambda f, x: remote(x_y, x_in.at[:, me_x], XX, me_d, f).start())
    x_in[:, me_x] = x_y[...]

    quarter = n_y * width
    arrived(w_in.at[pl.ds(0, n_y - 1)], WS)
    remote(w_in, w_mate, WMATE, mate, me_f).start()
    arrived(x_in.at[:, pl.ds(0, n_x - 1)], XX)
    full_x = x_in[...].reshape(wide, block)
    arrived(w_mate, WMATE)
    own_w = w_in[...].reshape(quarter, wide)
    other_w = w_mate[...].reshape(quarter, wide)
    w1 = jnp.where(core == 0, own_w, other_w)
    w2 = jnp.where(core == 0, other_w, own_w)
    preact = dot(w1, full_x)
    w1_t = w1.T
    w2_t = w2.T
    arrived(cot_in.at[pl.ds(0, n_y - 1)], COT)
    cot = cot_in[...].reshape(quarter, block).astype(F32)
    arrived(agg_in.at[pl.ds(0, n_feat - 1)], AGG)
    full_agg = agg_in[...].reshape(wide, block)
    preact += dot(w2, full_agg)
    s = jax.nn.sigmoid(preact)
    grad = (cot * s * (1.0 + preact * (1.0 - s))).astype(BF16)
    pair_out[0] = dot_t(grad, full_x)
    pair_out[1] = dot_t(grad, full_agg)
    remote(pair_out.at[1 - core], pair_in, PAIR, mate, me_f).start()

    part_out[0] = dot(w1_t, grad).astype(BF16).reshape(n_feat, width, block)
    part_out[1] = dot(w2_t, grad).astype(BF16).reshape(n_feat, width, block)
    part_in[:, me_f] = part_out[:, me_f]

    arrived(pair_in, PAIR)
    for half in range(2):
        lanes = slice(half * half_wide, (half + 1) * half_wide)
        summed = pair_out[core, :, lanes] + pair_in[:, lanes]
        grad_out[half] = summed.astype(BF16).reshape(n_y, width, half_wide)
        to_y(lambda f, y: remote(grad_out.at[half, y], grad_in.at[half, me_y], GRAD + half, me_d, f).start())
    grad_in[:, me_y] = grad_out[:, me_y]
    to_feat(lambda f, y: remote(part_out.at[1, f], part_in.at[1, me_f], SPREAD, me_d, f).start())
    to_feat(lambda f, y: remote(part_out.at[0, f], part_in.at[0, me_f], DIRECT, me_d, f).start())

    act_out[...] = (preact * s).astype(BF16).reshape(n_y, width, block)
    to_y(lambda f, y: remote(act_out.at[y], act_in.at[me_y], ACT, me_d, f).start())
    act_in[me_y] = act_out[me_y]

    for half in range(2):
        arrived(grad_in.at[half, pl.ds(0, n_y - 1)], GRAD + half)
        across_out[half] = jnp.sum(grad_in[half].astype(F32), axis=0).astype(BF16)
        to_z(lambda d, z: remote(across_out.at[half], across_in.at[half, me_z], ACROSS + half, d, me_f).start())
    across_in[:, me_z] = across_out[...]

    def quarters(which):
        return jnp.concatenate(
            [jnp.sum(part_in[which, y * n_x : (y + 1) * n_x].astype(F32), axis=0) for y in range(n_y)], axis=1
        )

    arrived(part_in.at[1, pl.ds(0, n_feat - 1)], SPREAD)
    spread = quarters(1) * inverse
    ends = split_dot_t(spread, edges[nodes:, :])
    back_out[0] = ends[:, :halo]
    back_out[1] = ends[:, halo:]
    remote(back_out.at[0], back_in.at[1], BACK, before, me_f).start()
    remote(back_out.at[1], back_in.at[0], BACK, after, me_f).start()

    gx = split_dot_t(spread, edges[:nodes, :])

    arrived(part_in.at[0, pl.ds(0, n_feat - 1)], DIRECT)
    gx += quarters(0)
    arrived(back_in, BACK)
    gx += split_dot_t(jnp.concatenate([back_in[0], back_in[1]], axis=1), chosen[...])
    gx_ref[...] = gx

    arrived(act_in.at[pl.ds(0, n_y - 1)], ACT)
    for y in range(n_y):
        act_ref[:, y * block : (y + 1) * block] = act_in[y]

    for half in range(2):
        arrived(across_in.at[half, pl.ds(0, n_z - 1)], ACROSS + half)
        summed = jnp.sum(across_in[half].astype(F32), axis=0) * (1.0 / math.sqrt(nodes * n_dom))
        sums[core, :, half * half_wide : (half + 1) * half_wide] = summed
    last = remote(sums.at[core], sums.at[core], LAST, mate, me_f)
    last.start()

    sent(halo_out, HALO)
    sent(w_in.at[pl.ds(0, n_y - 1)], WS)
    sent(w_in, WMATE)
    sent(x_y.at[pl.ds(0, n_y - 1)], XY)
    sent(x_in.at[:, pl.ds(0, n_x - 1)], XX)
    sent(cot_in.at[pl.ds(0, n_y - 1)], COT)
    sent(agg_in.at[pl.ds(0, n_feat - 1)], AGG)
    sent(pair_in, PAIR)
    sent(part_in.at[1, pl.ds(0, n_feat - 1)], SPREAD)
    sent(part_in.at[0, pl.ds(0, n_feat - 1)], DIRECT)
    sent(act_in.at[pl.ds(0, n_y - 1)], ACT)
    sent(back_out, BACK)
    for half in range(2):
        sent(grad_in.at[half, pl.ds(0, n_y - 1)], GRAD + half)
        sent(across_in.at[half, pl.ds(0, n_z - 1)], ACROSS + half)
    last.wait()
    gs_ref[...] = sums[0]
    gn_ref[...] = sums[1]


def hand_over(*refs):
    copies = [pltpu.make_async_copy(refs[i], refs[4 + i], refs[8].at[i]) for i in range(4)]
    for copy in copies:
        copy.start()
    for copy in copies:
        copy.wait()


def per_device(
    n_x, features, self_weight, neigh_weight, cotangent, neighbours, degrees, send_rows, send_count
):
    width, nodes = features.shape
    wide = self_weight.shape[0]
    slots = neighbours.shape[1]
    halo = send_rows.shape[1]
    n_dom = lax.axis_size("dom")
    n_feat = lax.axis_size("feat")
    n_y = n_feat // n_x
    block = nodes // n_y
    eb = min(256, 2 * halo)
    sizes = (n_dom, n_y, n_x, width, block, halo, slots, eb)
    vmem = pl.BlockSpec(memory_space=pltpu.VMEM)
    tile = lambda *lead: pltpu.VMEM((*lead, width, block), BF16)
    act, gx, gs, gn = pl.pallas_call(
        functools.partial(layer_kernel, sizes),
        out_shape=(
            pltpu.VMEM((width, nodes), BF16),
            pltpu.VMEM((width, nodes), F32),
            pltpu.VMEM((width, wide), F32),
            pltpu.VMEM((width, wide), F32),
        ),
        in_specs=[pl.BlockSpec(memory_space=pltpu.HBM)] * 7 + [pl.BlockSpec(memory_space=pltpu.SMEM)],
        out_specs=(vmem,) * 4,
        scratch_shapes=[
            pltpu.VMEM((2, width, wide), BF16),
            pltpu.VMEM((width, nodes), BF16),
            pltpu.VMEM((slots, nodes), jnp.int32),
            pltpu.VMEM((1, nodes), jnp.int32),
            pltpu.VMEM((2, halo), jnp.int32),
            pltpu.VMEM((width, nodes + 2 * halo), BF16),
            pltpu.VMEM((nodes, 2 * halo), BF16),
            pltpu.VMEM((nodes + 2 * halo, nodes), BF16),
            pltpu.VMEM((slots, nodes), jnp.int32),
            pltpu.VMEM((slots, nodes), jnp.int32),
            pltpu.VMEM((1, nodes), F32),
            pltpu.VMEM((2, width, halo), BF16),
            pltpu.VMEM((2, width, halo), BF16),
            tile(n_y), tile(n_y), tile(n_y, n_x),
            pltpu.VMEM((n_y, width, wide), BF16),
            pltpu.VMEM((n_y, width, wide), BF16),
            tile(n_y), tile(n_y),
            tile(n_y), tile(n_feat),
            tile(n_y), tile(n_y),
            tile(2, n_feat), tile(2, n_feat),
            pltpu.VMEM((2, n_y * width, wide), F32),
            pltpu.VMEM((n_y * width, wide), F32),
            pltpu.VMEM((2, n_y, width, wide // 2), BF16),
            pltpu.VMEM((2, n_y, width, wide // 2), BF16),
            pltpu.VMEM((2, width, halo), F32),
            pltpu.VMEM((2, width, halo), F32),
            pltpu.VMEM((2, width, wide // 2), BF16),
            pltpu.VMEM((2, n_dom // 2, width, wide // 2), BF16),
            pltpu.VMEM((2, width, wide), F32),
            pltpu.SemaphoreType.DMA((N_SEMS,)),
            pltpu.SemaphoreType.DMA((N_SEMS,)),
            pltpu.SemaphoreType.DMA((N_IN,)),
        ],
        compiler_params=pltpu.CompilerParams(
            collective_id=0, has_side_effects=True, vmem_limit_bytes=(64 * 1024 - 256) * 1024
        ),
    )(
        features, self_weight.T, neigh_weight.T, cotangent, neighbours.T, degrees.reshape(1, nodes),
        send_rows, send_count,
    )
    act, gx, gs, gn = pl.pallas_call(
        hand_over,
        out_shape=tuple(jax.ShapeDtypeStruct(a.shape, a.dtype) for a in (act, gx, gs, gn)),
        in_specs=[vmem] * 4,
        out_specs=(pl.BlockSpec(memory_space=pltpu.HBM),) * 4,
        scratch_shapes=[pltpu.SemaphoreType.DMA((4,))],
    )(*(pltpu.with_memory_space_constraint(a, pltpu.VMEM) for a in (act, gx, gs, gn)))
    return act, gx, gs.T, gn.T


def solution(mesh):
    n_x = 4 if mesh.shape["feat"] % 4 == 0 and mesh.shape["feat"] > 4 else 2
    return jax.shard_map(
        functools.partial(per_device, n_x),
        mesh=mesh,
        in_specs=(
            P("feat", "dom"),
            P(None, "feat"),
            P(None, "feat"),
            P("feat", "dom"),
            P("dom", None),
            P("dom"),
            P("dom", None),
            P("dom"),
        ),
        out_specs=(P("feat", "dom"), P("feat", "dom"), P(None, "feat"), P(None, "feat")),
        check_vma=False,
    )
```

```python
import functools
import math

import jax
import jax.numpy as jnp
from jax import lax
from jax.experimental import pallas as pl
from jax.experimental.pallas import tpu as pltpu
from jax.sharding import PartitionSpec as P

MESH = pl.DeviceIdType.MESH
BF16 = jnp.bfloat16
F32 = jnp.float32

HALO, XS, WS, WMATE, COT, AGG, ACT, DIRECT, SPREAD, PAIR, BACK, LAST, LAST_2, GRAD, GRAD_2, ACROSS, ACROSS_2, N_SEMS = range(18)
IN_X, IN_W1, IN_W2, IN_COT, IN_NB, IN_DEG, IN_ROWS, IN_COUNT, N_IN = range(9)


def dot(a, b):
    return jnp.dot(a, b, preferred_element_type=F32)


def dot_t(a, b):
    return lax.dot_general(a, b, (((1,), (1,)), ((), ())), preferred_element_type=F32)


def split_dot_t(a, b):
    high = a.astype(BF16)
    low = (a - high.astype(F32)).astype(BF16)
    both = dot_t(jnp.concatenate([high, low], axis=0), b)
    return both[: a.shape[0]] + both[a.shape[0] :]


def layer_kernel(
    sizes,
    x_hbm, w1_hbm, w2_hbm, cot_hbm, nb_hbm, deg_hbm, rows_hbm, count_hbm,
    act_ref, gx_ref, gs_ref, gn_ref,
    w_ref, cot_ref, nb_ref, deg_ref, rows_ref, count_ref,
    ext, chosen, edges, low_ref, unit_ref, inverse_ref,
    halo_out, halo_in, x_out, x_in, w_in, w_mate, cot_out, cot_in, agg_out, agg_in,
    act_out, act_in, part_out, part_in, pair_out, pair_in, grad_out, grad_in, back_out, back_in,
    across_out, across_in, sums,
    send_sem, recv_sem, in_sem,
):
    n_dom, n_feat, n_b, width, block, halo, slots, eb = sizes
    n_q = n_feat // n_b
    n_z = n_dom // 2
    nodes = n_b * block
    wide = w1_hbm.shape[1]
    half_wide = wide // 2
    me_d = lax.axis_index("dom")
    me_f = lax.axis_index("feat")
    me_b = me_f % n_b
    me_q = me_f // n_b
    me_z = me_d // 2
    core = me_d % 2
    mate = me_d + 1 - 2 * core
    before = lax.rem(me_d + n_dom - 1, n_dom)
    after = lax.rem(me_d + 1, n_dom)
    far = jnp.where(core == 0, before, after)

    loads = {}
    for which, src, dst in (
        (IN_X, x_hbm, ext.at[:, pl.ds(0, nodes)]), (IN_ROWS, rows_hbm, rows_ref), (IN_COUNT, count_hbm, count_ref),
        (IN_NB, nb_hbm, nb_ref),
        (IN_DEG, deg_hbm, deg_ref), (IN_W1, w1_hbm, w_ref.at[0]), (IN_W2, w2_hbm, w_ref.at[1]), (IN_COT, cot_hbm, cot_ref),
    ):
        loads[which] = pltpu.make_async_copy(src, dst, in_sem.at[which])
        loads[which].start()

    def remote(src, dst, which, dom, feat):
        return pltpu.make_async_remote_copy(
            src_ref=src, dst_ref=dst, send_sem=send_sem.at[which], recv_sem=recv_sem.at[which],
            device_id={"dom": dom, "feat": feat}, device_id_type=MESH,
        )

    def arrived(ref, which):
        remote(ref, ref, which, me_d, me_f).wait_recv()

    def sent(ref, which):
        remote(ref, ref, which, me_d, me_f).wait_send()

    def each(count, body):
        def step(i, carry):
            body(i)
            return carry
        lax.fori_loop(0, count, step, 0)

    def from_half(i, count):
        return 1 + lax.rem(i + max(3 * count // 8 - 1, 0), count - 1)

    def to_feat(body):
        def one(i):
            other = lax.rem(me_f + from_half(i, n_feat), n_feat)
            body(other, lax.rem(other, n_b))
        each(n_feat - 1, one)

    def to_group(body):
        def one(i):
            other = lax.rem(me_b + from_half(i, n_b), n_b)
            body(me_q * n_b + other, other)
        each(n_b - 1, one)

    barrier = pltpu.get_barrier_semaphore()

    def greet(dom, feat):
        pl.semaphore_signal(barrier, inc=1, device_id={"dom": dom, "feat": feat}, device_id_type=MESH)

    def to_z(body):
        def one(i):
            other = lax.rem(me_z + from_half(i, n_z), n_z)
            body(other * 2 + core, other)
        each(n_z - 1, one)

    greet(far, me_f)
    to_z(lambda d, z: greet(d, me_f))
    to_feat(lambda f, b: greet(me_d, f))
    greet(mate, me_f)

    slot_id = lax.broadcasted_iota(jnp.int32, (1, 2 * halo), 1)
    loads[IN_COUNT].wait()
    limit = jnp.where(slot_id < halo, count_ref[0], count_ref[1] + halo)
    loads[IN_ROWS].wait()
    rows = jnp.concatenate([rows_ref[0:1, :], rows_ref[1:2, :]], axis=1)
    rows = jnp.where(slot_id < limit, rows, -1)
    node_id = lax.broadcasted_iota(jnp.int32, (nodes, 2 * halo), 0)
    chosen[...] = jnp.where(node_id == rows, 1.0, 0.0).astype(BF16)
    loads[IN_X].wait()
    x = ext[:, :nodes]
    picked = dot(x, chosen[...]).astype(BF16)
    halo_out[0] = picked[:, :halo]
    halo_out[1] = picked[:, halo:]
    for b in range(n_b):
        x_out[b] = x[:, b * block : (b + 1) * block]
    x_in[me_f] = x_out[me_b]

    loads[IN_DEG].wait()
    loads[IN_NB].wait()
    degree = deg_ref[...]
    slot = lax.broadcasted_iota(jnp.int32, (slots, nodes), 0)
    nb = nb_ref[...]
    low_ref[...] = jnp.where(slot < degree, nb % eb, -1)
    unit_ref[...] = jnp.left_shift(jnp.ones_like(nb), 6 * (nb // eb))
    inverse = 1.0 / degree.astype(F32)
    inverse_ref[...] = inverse

    n_pairs = n_b // 2
    pairs = [lax.rem(me_b // 2 + off, n_pairs) for off in sorted(range(n_pairs), key=lambda o: -min(o, n_pairs - o))]

    def pair_lanes(pair):
        return pl.ds(pl.multiple_of(pair * 2 * block, 2 * block), 2 * block)

    def count_edges(pair):
        rows_once = min(128, eb)

        def one(t):
            lanes = pl.ds(pl.multiple_of((pair * 2 + t % 2) * block, block), block)
            base = (t // 2) * rows_once
            low = low_ref[:, lanes] - base
            unit = unit_ref[:, lanes]
            known = lax.broadcasted_iota(jnp.int32, (rows_once, block), 0)
            total = jnp.zeros((rows_once, block), jnp.int32)
            for k in range(slots):
                total = total + jnp.where(known == low[k : k + 1, :], unit[k : k + 1, :], 0)
            for high in range((nodes + 2 * halo) // eb):
                count = ((total >> (6 * high)) & 63).astype(F32).astype(BF16)
                edges[pl.ds(pl.multiple_of(high * eb + base, rows_once), rows_once), lanes] = count

        each(2 * eb // rows_once, one)

    for pair in pairs[:2]:
        count_edges(pair)

    loads[IN_COT].wait()
    for b in range(n_b):
        cot_out[b] = cot_ref[:, b * block : (b + 1) * block]
    cot_in[me_b] = cot_out[me_b]
    loads[IN_W1].wait()
    loads[IN_W2].wait()
    w_in[me_b] = w_ref[core]

    pl.semaphore_wait(barrier, n_feat - 1 + n_z - 1 + 2)

    remote(halo_out.at[0], halo_in.at[1], HALO, before, me_f).start()
    remote(halo_out.at[1], halo_in.at[0], HALO, after, me_f).start()
    to_group(lambda f, b: remote(w_ref.at[core], w_in.at[me_b], WS, me_d, f).start())
    to_group(lambda f, b: remote(cot_out.at[b], cot_in.at[me_b], COT, me_d, f).start())
    to_feat(lambda f, b: remote(x_out.at[b], x_in.at[me_f], XS, me_d, f).start())

    for pair in pairs[2:]:
        count_edges(pair)
    arrived(halo_in, HALO)
    ext[:, nodes : nodes + halo] = halo_in[0]
    ext[:, nodes + halo :] = halo_in[1]
    for pair in pairs:
        lanes = pair_lanes(pair)
        mean = (dot(ext[...], edges[:, lanes]) * inverse_ref[:, lanes]).astype(BF16)
        agg_out[pair * 2] = mean[:, :block]
        agg_out[pair * 2 + 1] = mean[:, block:]

        def give(i):
            b = pair * 2 + i // n_q
            other = lax.rem(me_q + i + n_q // 2, n_q) * n_b + b

            @pl.when(other != me_f)
            def _():
                remote(agg_out.at[b], agg_in.at[me_f], AGG, me_d, other).start()

        each(2 * n_q, give)
    agg_in[me_f] = agg_out[me_b]

    quarter = n_b * width
    arrived(w_in.at[pl.ds(0, n_b - 1)], WS)
    remote(w_in, w_mate, WMATE, mate, me_f).start()
    arrived(x_in.at[pl.ds(0, n_feat - 1)], XS)
    full_x = x_in[...].reshape(wide, block)
    arrived(w_mate, WMATE)
    own_w = w_in[...].reshape(quarter, wide)
    other_w = w_mate[...].reshape(quarter, wide)
    w1 = jnp.where(core == 0, own_w, other_w)
    w2 = jnp.where(core == 0, other_w, own_w)
    preact = dot(w1, full_x)
    arrived(cot_in.at[pl.ds(0, n_b - 1)], COT)
    cot = cot_in[...].reshape(quarter, block).astype(F32)
    arrived(agg_in.at[pl.ds(0, n_feat - 1)], AGG)
    full_agg = agg_in[...].reshape(wide, block)
    preact += dot(w2, full_agg)
    s = jax.nn.sigmoid(preact)
    grad = (cot * s * (1.0 + preact * (1.0 - s))).astype(BF16)
    pair_out[...] = dot_t(grad, jnp.where(core == 0, full_agg, full_x))
    remote(pair_out, pair_in, PAIR, mate, me_f).start()
    weight_grad = dot_t(grad, jnp.where(core == 0, full_x, full_agg))

    w1_t = w1.T
    w2_t = w2.T
    part_out[0] = dot(w1_t, grad).astype(BF16).reshape(n_feat, width, block)
    part_out[1] = dot(w2_t, grad).astype(BF16).reshape(n_feat, width, block)
    part_in[:, me_f] = part_out[:, me_f]

    arrived(pair_in, PAIR)
    for half in range(2):
        lanes = slice(half * half_wide, (half + 1) * half_wide)
        summed = weight_grad[:, lanes] + pair_in[:, lanes]
        grad_out[half] = summed.astype(BF16).reshape(n_b, width, half_wide)
        to_group(lambda f, b: remote(grad_out.at[half, b], grad_in.at[half, me_b], GRAD + half, me_d, f).start())
    grad_in[:, me_b] = grad_out[:, me_b]
    to_feat(lambda f, b: remote(part_out.at[1, f], part_in.at[1, me_f], SPREAD, me_d, f).start())
    to_feat(lambda f, b: remote(part_out.at[0, f], part_in.at[0, me_f], DIRECT, me_d, f).start())

    act_out[...] = (preact * s).astype(BF16).reshape(n_b, width, block)
    to_group(lambda f, b: remote(act_out.at[b], act_in.at[me_b], ACT, me_d, f).start())
    act_in[me_b] = act_out[me_b]

    for half in range(2):
        arrived(grad_in.at[half, pl.ds(0, n_b - 1)], GRAD + half)
        across_out[half] = jnp.sum(grad_in[half].astype(F32), axis=0).astype(BF16)
        to_z(lambda d, z: remote(across_out.at[half], across_in.at[half, me_z], ACROSS + half, d, me_f).start())
    across_in[:, me_z] = across_out[...]

    def quarters(which):
        total = jnp.sum(part_in[which].reshape(n_q, n_b, width, block).astype(F32), axis=0)
        return jnp.concatenate([total[b] for b in range(n_b)], axis=1)

    arrived(part_in.at[1, pl.ds(0, n_feat - 1)], SPREAD)
    spread = quarters(1) * inverse
    ends = split_dot_t(spread, edges[nodes:, :])
    back_out[0] = ends[:, :halo]
    back_out[1] = ends[:, halo:]
    remote(back_out.at[0], back_in.at[1], BACK, before, me_f).start()
    remote(back_out.at[1], back_in.at[0], BACK, after, me_f).start()

    gx = split_dot_t(spread, edges[:nodes, :])

    arrived(part_in.at[0, pl.ds(0, n_feat - 1)], DIRECT)
    gx += quarters(0)
    arrived(back_in, BACK)
    gx += split_dot_t(jnp.concatenate([back_in[0], back_in[1]], axis=1), chosen[...])
    gx_ref[...] = gx

    arrived(act_in.at[pl.ds(0, n_b - 1)], ACT)
    for b in range(n_b):
        act_ref[:, b * block : (b + 1) * block] = act_in[b]

    lasts = []
    for half in range(2):
        arrived(across_in.at[half, pl.ds(0, n_z - 1)], ACROSS + half)
        summed = jnp.sum(across_in[half].astype(F32), axis=0) * (1.0 / math.sqrt(nodes * n_dom))
        sums[core, half] = summed
        lasts.append(remote(sums.at[core, half], sums.at[core, half], LAST + half, mate, me_f))
        lasts[half].start()

    sent(halo_out, HALO)
    sent(w_in.at[pl.ds(0, n_b - 1)], WS)
    sent(w_in, WMATE)
    sent(x_in.at[pl.ds(0, n_feat - 1)], XS)
    sent(cot_in.at[pl.ds(0, n_b - 1)], COT)
    sent(agg_in.at[pl.ds(0, n_feat - 1)], AGG)
    sent(pair_in, PAIR)
    sent(part_in.at[1, pl.ds(0, n_feat - 1)], SPREAD)
    sent(part_in.at[0, pl.ds(0, n_feat - 1)], DIRECT)
    sent(act_in.at[pl.ds(0, n_b - 1)], ACT)
    sent(back_out, BACK)
    for half in range(2):
        sent(grad_in.at[half, pl.ds(0, n_b - 1)], GRAD + half)
        sent(across_in.at[half, pl.ds(0, n_z - 1)], ACROSS + half)
    for half in range(2):
        lanes = slice(half * half_wide, (half + 1) * half_wide)
        lasts[half].wait()
        gs_ref[:, lanes] = sums[0, half]
        gn_ref[:, lanes] = sums[1, half]


def hand_over(*refs):
    copies = [pltpu.make_async_copy(refs[i], refs[4 + i], refs[8].at[i]) for i in range(4)]
    for copy in copies:
        copy.start()
    for copy in copies:
        copy.wait()


def per_device(
    features, self_weight, neigh_weight, cotangent, neighbours, degrees, send_rows, send_count
):
    width, nodes = features.shape
    wide = self_weight.shape[0]
    slots = neighbours.shape[1]
    halo = send_rows.shape[1]
    n_dom = lax.axis_size("dom")
    n_feat = lax.axis_size("feat")
    block = 128
    n_b = nodes // block
    eb = min(256, 2 * halo)
    sizes = (n_dom, n_feat, n_b, width, block, halo, slots, eb)
    vmem = pl.BlockSpec(memory_space=pltpu.VMEM)
    tile = lambda *lead: pltpu.VMEM((*lead, width, block), BF16)
    act, gx, gs, gn = pl.pallas_call(
        functools.partial(layer_kernel, sizes),
        out_shape=(
            pltpu.VMEM((width, nodes), BF16),
            pltpu.VMEM((width, nodes), F32),
            pltpu.VMEM((width, wide), F32),
            pltpu.VMEM((width, wide), F32),
        ),
        in_specs=[pl.BlockSpec(memory_space=pltpu.HBM)] * 8,
        out_specs=(vmem,) * 4,
        scratch_shapes=[
            pltpu.VMEM((2, width, wide), BF16),
            pltpu.VMEM((width, nodes), BF16),
            pltpu.VMEM((slots, nodes), jnp.int32),
            pltpu.VMEM((1, nodes), jnp.int32),
            pltpu.VMEM((2, halo), jnp.int32),
            pltpu.SMEM((2,), jnp.int32),
            pltpu.VMEM((width, nodes + 2 * halo), BF16),
            pltpu.VMEM((nodes, 2 * halo), BF16),
            pltpu.VMEM((nodes + 2 * halo, nodes), BF16),
            pltpu.VMEM((slots, nodes), jnp.int32),
            pltpu.VMEM((slots, nodes), jnp.int32),
            pltpu.VMEM((1, nodes), F32),
            pltpu.VMEM((2, width, halo), BF16),
            pltpu.VMEM((2, width, halo), BF16),
            tile(n_b), tile(n_feat),
            pltpu.VMEM((n_b, width, wide), BF16),
            pltpu.VMEM((n_b, width, wide), BF16),
            tile(n_b), tile(n_b),
            tile(n_b), tile(n_feat),
            tile(n_b), tile(n_b),
            tile(2, n_feat), tile(2, n_feat),
            pltpu.VMEM((n_b * width, wide), F32),
            pltpu.VMEM((n_b * width, wide), F32),
            pltpu.VMEM((2, n_b, width, wide // 2), BF16),
            pltpu.VMEM((2, n_b, width, wide // 2), BF16),
            pltpu.VMEM((2, width, halo), F32),
            pltpu.VMEM((2, width, halo), F32),
            pltpu.VMEM((2, width, wide // 2), BF16),
            pltpu.VMEM((2, n_dom // 2, width, wide // 2), BF16),
            pltpu.VMEM((2, 2, width, wide // 2), F32),
            pltpu.SemaphoreType.DMA((N_SEMS,)),
            pltpu.SemaphoreType.DMA((N_SEMS,)),
            pltpu.SemaphoreType.DMA((N_IN,)),
        ],
        compiler_params=pltpu.CompilerParams(
            collective_id=0, has_side_effects=True, vmem_limit_bytes=(64 * 1024 - 256) * 1024
        ),
    )(
        features, self_weight.T, neigh_weight.T, cotangent, neighbours.T, degrees.reshape(1, nodes),
        send_rows, send_count,
    )
    act, gx, gs, gn = pl.pallas_call(
        hand_over,
        out_shape=tuple(jax.ShapeDtypeStruct(a.shape, a.dtype) for a in (act, gx, gs, gn)),
        in_specs=[vmem] * 4,
        out_specs=(pl.BlockSpec(memory_space=pltpu.HBM),) * 4,
        scratch_shapes=[pltpu.SemaphoreType.DMA((4,))],
    )(*(pltpu.with_memory_space_constraint(a, pltpu.VMEM) for a in (act, gx, gs, gn)))
    return act, gx, gs.T, gn.T


def solution(mesh):
    return jax.shard_map(
        per_device,
        mesh=mesh,
        in_specs=(
            P("feat", "dom"),
            P(None, "feat"),
            P(None, "feat"),
            P("feat", "dom"),
            P("dom", None),
            P("dom"),
            P("dom", None),
            P("dom"),
        ),
        out_specs=(P("feat", "dom"), P("feat", "dom"), P(None, "feat"), P(None, "feat")),
        check_vma=False,
    )
```

```python
import functools
import math

import jax
import jax.numpy as jnp
from jax import lax
from jax.experimental import pallas as pl
from jax.experimental.pallas import tpu as pltpu
from jax.sharding import PartitionSpec as P

MESH = pl.DeviceIdType.MESH
BF16 = jnp.bfloat16
F32 = jnp.float32

HALO, XS, WS, WMATE, COT, AGG, ACT, DIRECT, SPREAD, PAIR, BACK, LAST, LAST_2, GRAD, GRAD_2, ACROSS, ACROSS_2, N_SEMS = range(18)
IN_X, IN_W1, IN_W2, IN_COT, IN_NB, IN_DEG, IN_ROWS, IN_COUNT, N_IN = range(9)


def dot(a, b):
    return jnp.dot(a, b, preferred_element_type=F32)


def dot_t(a, b):
    return lax.dot_general(a, b, (((1,), (1,)), ((), ())), preferred_element_type=F32)


def split_dot_t(a, b):
    high = a.astype(BF16)
    low = (a - high.astype(F32)).astype(BF16)
    both = dot_t(jnp.concatenate([high, low], axis=0), b)
    return both[: a.shape[0]] + both[a.shape[0] :]


def layer_kernel(
    sizes,
    x_hbm, w1_hbm, w2_hbm, cot_hbm, nb_hbm, deg_hbm, rows_hbm, count_hbm,
    act_ref, gx_ref, gs_ref, gn_ref,
    w_ref, cot_ref, nb_ref, deg_ref, rows_ref, count_ref,
    ext, chosen, edges, low_ref, unit_ref, inverse_ref,
    halo_out, halo_in, x_out, x_in, w_in, w_mate, cot_out, cot_in, agg_out, agg_in,
    act_out, act_in, part_out, part_in, pair_out, pair_in, grad_out, grad_in, back_out, back_in,
    across_out, across_in, sums,
    send_sem, recv_sem, in_sem,
):
    n_dom, n_feat, n_b, width, block, halo, slots, eb = sizes
    n_q = n_feat // n_b
    n_z = n_dom // 2
    nodes = n_b * block
    wide = w1_hbm.shape[1]
    half_wide = wide // 2
    me_d = lax.axis_index("dom")
    me_f = lax.axis_index("feat")
    me_b = me_f % n_b
    me_q = me_f // n_b
    me_z = me_d // 2
    core = me_d % 2
    mate = me_d + 1 - 2 * core
    before = lax.rem(me_d + n_dom - 1, n_dom)
    after = lax.rem(me_d + 1, n_dom)
    far = jnp.where(core == 0, before, after)

    loads = {}
    for which, src, dst in (
        (IN_X, x_hbm, ext.at[:, pl.ds(0, nodes)]), (IN_ROWS, rows_hbm, rows_ref), (IN_COUNT, count_hbm, count_ref),
        (IN_NB, nb_hbm, nb_ref),
        (IN_DEG, deg_hbm, deg_ref), (IN_W1, w1_hbm, w_ref.at[0]), (IN_W2, w2_hbm, w_ref.at[1]), (IN_COT, cot_hbm, cot_ref),
    ):
        loads[which] = pltpu.make_async_copy(src, dst, in_sem.at[which])
        loads[which].start()

    def remote(src, dst, which, dom, feat):
        return pltpu.make_async_remote_copy(
            src_ref=src, dst_ref=dst, send_sem=send_sem.at[which], recv_sem=recv_sem.at[which],
            device_id={"dom": dom, "feat": feat}, device_id_type=MESH,
        )

    def arrived(ref, which):
        remote(ref, ref, which, me_d, me_f).wait_recv()

    def sent(ref, which):
        remote(ref, ref, which, me_d, me_f).wait_send()

    def each(count, body):
        def step(i, carry):
            body(i)
            return carry
        lax.fori_loop(0, count, step, 0)

    def from_half(i, count):
        return count // 2 + (1 - 2 * (i % 2)) * ((i + 1) // 2)

    def to_feat(body):
        def one(i):
            other = lax.rem(me_f + from_half(i, n_feat), n_feat)
            body(other, lax.rem(other, n_b))
        each(n_feat - 1, one)

    def to_group(body):
        def one(i):
            other = lax.rem(me_b + from_half(i, n_b), n_b)
            body(me_q * n_b + other, other)
        each(n_b - 1, one)

    barrier = pltpu.get_barrier_semaphore()

    def greet(dom, feat):
        pl.semaphore_signal(barrier, inc=1, device_id={"dom": dom, "feat": feat}, device_id_type=MESH)

    def to_z(body):
        def one(i):
            other = lax.rem(me_z + from_half(i, n_z), n_z)
            body(other * 2 + core, other)
        each(n_z - 1, one)

    greet(far, me_f)
    to_z(lambda d, z: greet(d, me_f))
    to_feat(lambda f, b: greet(me_d, f))
    greet(mate, me_f)

    slot_id = lax.broadcasted_iota(jnp.int32, (1, 2 * halo), 1)
    loads[IN_COUNT].wait()
    limit = jnp.where(slot_id < halo, count_ref[0], count_ref[1] + halo)
    loads[IN_ROWS].wait()
    rows = jnp.concatenate([rows_ref[0:1, :], rows_ref[1:2, :]], axis=1)
    rows = jnp.where(slot_id < limit, rows, -1)
    node_id = lax.broadcasted_iota(jnp.int32, (nodes, 2 * halo), 0)
    chosen[...] = jnp.where(node_id == rows, 1.0, 0.0).astype(BF16)
    loads[IN_X].wait()
    x = ext[:, :nodes]
    picked = dot(x, chosen[...]).astype(BF16)
    halo_out[0] = picked[:, :halo]
    halo_out[1] = picked[:, halo:]
    for b in range(n_b):
        x_out[b] = x[:, b * block : (b + 1) * block]
    x_in[me_f] = x_out[me_b]

    loads[IN_DEG].wait()
    loads[IN_NB].wait()
    degree = deg_ref[...]
    slot = lax.broadcasted_iota(jnp.int32, (slots, nodes), 0)
    nb = nb_ref[...]
    low_ref[...] = jnp.where(slot < degree, nb % eb, -1)
    unit_ref[...] = jnp.left_shift(jnp.ones_like(nb), 6 * (nb // eb))
    inverse = 1.0 / degree.astype(F32)
    inverse_ref[...] = inverse

    n_pairs = n_b // 2
    pairs = [lax.rem(me_b // 2 + off, n_pairs) for off in sorted(range(n_pairs), key=lambda o: -min(o, n_pairs - o))]

    def pair_lanes(pair):
        return pl.ds(pl.multiple_of(pair * 2 * block, 2 * block), 2 * block)

    def count_edges(pair):
        rows_once = min(128, eb)

        def one(t):
            lanes = pl.ds(pl.multiple_of((pair * 2 + t % 2) * block, block), block)
            base = (t // 2) * rows_once
            low = low_ref[:, lanes] - base
            unit = unit_ref[:, lanes]
            known = lax.broadcasted_iota(jnp.int32, (rows_once, block), 0)
            total = jnp.zeros((rows_once, block), jnp.int32)
            for k in range(slots):
                total = total + jnp.where(known == low[k : k + 1, :], unit[k : k + 1, :], 0)
            for high in range((nodes + 2 * halo) // eb):
                count = ((total >> (6 * high)) & 63).astype(F32).astype(BF16)
                edges[pl.ds(pl.multiple_of(high * eb + base, rows_once), rows_once), lanes] = count

        each(2 * eb // rows_once, one)

    for pair in pairs[:2]:
        count_edges(pair)

    loads[IN_COT].wait()
    for b in range(n_b):
        cot_out[b] = cot_ref[:, b * block : (b + 1) * block]
    cot_in[me_b] = cot_out[me_b]
    loads[IN_W1].wait()
    loads[IN_W2].wait()
    w_in[me_b] = w_ref[core]

    pl.semaphore_wait(barrier, n_feat - 1 + n_z - 1 + 2)

    remote(halo_out.at[0], halo_in.at[1], HALO, before, me_f).start()
    remote(halo_out.at[1], halo_in.at[0], HALO, after, me_f).start()
    to_group(lambda f, b: remote(w_ref.at[core], w_in.at[me_b], WS, me_d, f).start())
    to_group(lambda f, b: remote(cot_out.at[b], cot_in.at[me_b], COT, me_d, f).start())
    to_feat(lambda f, b: remote(x_out.at[b], x_in.at[me_f], XS, me_d, f).start())

    for pair in pairs[2:]:
        count_edges(pair)
    arrived(halo_in, HALO)
    ext[:, nodes : nodes + halo] = halo_in[0]
    ext[:, nodes + halo :] = halo_in[1]
    for pair in pairs:
        lanes = pair_lanes(pair)
        mean = (dot(ext[...], edges[:, lanes]) * inverse_ref[:, lanes]).astype(BF16)
        agg_out[pair * 2] = mean[:, :block]
        agg_out[pair * 2 + 1] = mean[:, block:]

        def give(i):
            b = pair * 2 + i // n_q
            other = lax.rem(me_q + i + n_q // 2, n_q) * n_b + b

            @pl.when(other != me_f)
            def _():
                remote(agg_out.at[b], agg_in.at[me_f], AGG, me_d, other).start()

        each(2 * n_q, give)
    agg_in[me_f] = agg_out[me_b]

    quarter = n_b * width
    arrived(w_in.at[pl.ds(0, n_b - 1)], WS)
    remote(w_in, w_mate, WMATE, mate, me_f).start()
    arrived(x_in.at[pl.ds(0, n_feat - 1)], XS)
    full_x = x_in[...].reshape(wide, block)
    arrived(w_mate, WMATE)
    own_w = w_in[...].reshape(quarter, wide)
    other_w = w_mate[...].reshape(quarter, wide)
    w1 = jnp.where(core == 0, own_w, other_w)
    w2 = jnp.where(core == 0, other_w, own_w)
    preact = dot(w1, full_x)
    arrived(cot_in.at[pl.ds(0, n_b - 1)], COT)
    cot = cot_in[...].reshape(quarter, block).astype(F32)
    arrived(agg_in.at[pl.ds(0, n_feat - 1)], AGG)
    full_agg = agg_in[...].reshape(wide, block)
    preact += dot(w2, full_agg)
    s = jax.nn.sigmoid(preact)
    grad = (cot * s * (1.0 + preact * (1.0 - s))).astype(BF16)
    pair_out[...] = dot_t(grad, jnp.where(core == 0, full_agg, full_x))
    remote(pair_out, pair_in, PAIR, mate, me_f).start()
    weight_grad = dot_t(grad, jnp.where(core == 0, full_x, full_agg))

    w1_t = w1.T
    w2_t = w2.T
    part_out[0] = dot(w1_t, grad).astype(BF16).reshape(n_feat, width, block)
    part_out[1] = dot(w2_t, grad).astype(BF16).reshape(n_feat, width, block)
    part_in[:, me_f] = part_out[:, me_f]

    arrived(pair_in, PAIR)
    for half in range(2):
        lanes = slice(half * half_wide, (half + 1) * half_wide)
        summed = weight_grad[:, lanes] + pair_in[:, lanes]
        grad_out[half] = summed.astype(BF16).reshape(n_b, width, half_wide)
        to_group(lambda f, b: remote(grad_out.at[half, b], grad_in.at[half, me_b], GRAD + half, me_d, f).start())
    grad_in[:, me_b] = grad_out[:, me_b]
    to_feat(lambda f, b: remote(part_out.at[1, f], part_in.at[1, me_f], SPREAD, me_d, f).start())
    to_feat(lambda f, b: remote(part_out.at[0, f], part_in.at[0, me_f], DIRECT, me_d, f).start())

    act_out[...] = (preact * s).astype(BF16).reshape(n_b, width, block)
    to_group(lambda f, b: remote(act_out.at[b], act_in.at[me_b], ACT, me_d, f).start())
    act_in[me_b] = act_out[me_b]

    for half in range(2):
        arrived(grad_in.at[half, pl.ds(0, n_b - 1)], GRAD + half)
        across_out[half] = jnp.sum(grad_in[half].astype(F32), axis=0).astype(BF16)
        to_z(lambda d, z: remote(across_out.at[half], across_in.at[half, me_z], ACROSS + half, d, me_f).start())
    across_in[:, me_z] = across_out[...]

    def quarters(which):
        total = jnp.sum(part_in[which].reshape(n_q, n_b, width, block).astype(F32), axis=0)
        return jnp.concatenate([total[b] for b in range(n_b)], axis=1)

    arrived(part_in.at[1, pl.ds(0, n_feat - 1)], SPREAD)
    spread = quarters(1) * inverse
    ends = split_dot_t(spread, edges[nodes:, :])
    back_out[0] = ends[:, :halo]
    back_out[1] = ends[:, halo:]
    remote(back_out.at[0], back_in.at[1], BACK, before, me_f).start()
    remote(back_out.at[1], back_in.at[0], BACK, after, me_f).start()

    gx = split_dot_t(spread, edges[:nodes, :])

    arrived(part_in.at[0, pl.ds(0, n_feat - 1)], DIRECT)
    gx += quarters(0)
    arrived(back_in, BACK)
    gx += split_dot_t(jnp.concatenate([back_in[0], back_in[1]], axis=1), chosen[...])
    gx_ref[...] = gx

    arrived(act_in.at[pl.ds(0, n_b - 1)], ACT)
    for b in range(n_b):
        act_ref[:, b * block : (b + 1) * block] = act_in[b]

    lasts = []
    for half in range(2):
        arrived(across_in.at[half, pl.ds(0, n_z - 1)], ACROSS + half)
        summed = jnp.sum(across_in[half].astype(F32), axis=0) * (1.0 / math.sqrt(nodes * n_dom))
        sums[core, half] = summed
        lasts.append(remote(sums.at[core, half], sums.at[core, half], LAST + half, mate, me_f))
        lasts[half].start()

    sent(halo_out, HALO)
    sent(w_in.at[pl.ds(0, n_b - 1)], WS)
    sent(w_in, WMATE)
    sent(x_in.at[pl.ds(0, n_feat - 1)], XS)
    sent(cot_in.at[pl.ds(0, n_b - 1)], COT)
    sent(agg_in.at[pl.ds(0, n_feat - 1)], AGG)
    sent(pair_in, PAIR)
    sent(part_in.at[1, pl.ds(0, n_feat - 1)], SPREAD)
    sent(part_in.at[0, pl.ds(0, n_feat - 1)], DIRECT)
    sent(act_in.at[pl.ds(0, n_b - 1)], ACT)
    sent(back_out, BACK)
    for half in range(2):
        sent(grad_in.at[half, pl.ds(0, n_b - 1)], GRAD + half)
        sent(across_in.at[half, pl.ds(0, n_z - 1)], ACROSS + half)
    for half in range(2):
        lanes = slice(half * half_wide, (half + 1) * half_wide)
        lasts[half].wait()
        gs_ref[:, lanes] = sums[0, half]
        gn_ref[:, lanes] = sums[1, half]


def hand_over(*refs):
    copies = [pltpu.make_async_copy(refs[i], refs[4 + i], refs[8].at[i]) for i in range(4)]
    for copy in copies:
        copy.start()
    for copy in copies:
        copy.wait()


def per_device(
    features, self_weight, neigh_weight, cotangent, neighbours, degrees, send_rows, send_count
):
    width, nodes = features.shape
    wide = self_weight.shape[0]
    slots = neighbours.shape[1]
    halo = send_rows.shape[1]
    n_dom = lax.axis_size("dom")
    n_feat = lax.axis_size("feat")
    block = 128
    n_b = nodes // block
    eb = min(256, 2 * halo)
    sizes = (n_dom, n_feat, n_b, width, block, halo, slots, eb)
    vmem = pl.BlockSpec(memory_space=pltpu.VMEM)
    tile = lambda *lead: pltpu.VMEM((*lead, width, block), BF16)
    act, gx, gs, gn = pl.pallas_call(
        functools.partial(layer_kernel, sizes),
        out_shape=(
            pltpu.VMEM((width, nodes), BF16),
            pltpu.VMEM((width, nodes), F32),
            pltpu.VMEM((width, wide), F32),
            pltpu.VMEM((width, wide), F32),
        ),
        in_specs=[pl.BlockSpec(memory_space=pltpu.HBM)] * 8,
        out_specs=(vmem,) * 4,
        scratch_shapes=[
            pltpu.VMEM((2, width, wide), BF16),
            pltpu.VMEM((width, nodes), BF16),
            pltpu.VMEM((slots, nodes), jnp.int32),
            pltpu.VMEM((1, nodes), jnp.int32),
            pltpu.VMEM((2, halo), jnp.int32),
            pltpu.SMEM((2,), jnp.int32),
            pltpu.VMEM((width, nodes + 2 * halo), BF16),
            pltpu.VMEM((nodes, 2 * halo), BF16),
            pltpu.VMEM((nodes + 2 * halo, nodes), BF16),
            pltpu.VMEM((slots, nodes), jnp.int32),
            pltpu.VMEM((slots, nodes), jnp.int32),
            pltpu.VMEM((1, nodes), F32),
            pltpu.VMEM((2, width, halo), BF16),
            pltpu.VMEM((2, width, halo), BF16),
            tile(n_b), tile(n_feat),
            pltpu.VMEM((n_b, width, wide), BF16),
            pltpu.VMEM((n_b, width, wide), BF16),
            tile(n_b), tile(n_b),
            tile(n_b), tile(n_feat),
            tile(n_b), tile(n_b),
            tile(2, n_feat), tile(2, n_feat),
            pltpu.VMEM((n_b * width, wide), F32),
            pltpu.VMEM((n_b * width, wide), F32),
            pltpu.VMEM((2, n_b, width, wide // 2), BF16),
            pltpu.VMEM((2, n_b, width, wide // 2), BF16),
            pltpu.VMEM((2, width, halo), F32),
            pltpu.VMEM((2, width, halo), F32),
            pltpu.VMEM((2, width, wide // 2), BF16),
            pltpu.VMEM((2, n_dom // 2, width, wide // 2), BF16),
            pltpu.VMEM((2, 2, width, wide // 2), F32),
            pltpu.SemaphoreType.DMA((N_SEMS,)),
            pltpu.SemaphoreType.DMA((N_SEMS,)),
            pltpu.SemaphoreType.DMA((N_IN,)),
        ],
        compiler_params=pltpu.CompilerParams(
            collective_id=0, has_side_effects=True, vmem_limit_bytes=(64 * 1024 - 256) * 1024
        ),
    )(
        features, self_weight.T, neigh_weight.T, cotangent, neighbours.T, degrees.reshape(1, nodes),
        send_rows, send_count,
    )
    act, gx, gs, gn = pl.pallas_call(
        hand_over,
        out_shape=tuple(jax.ShapeDtypeStruct(a.shape, a.dtype) for a in (act, gx, gs, gn)),
        in_specs=[vmem] * 4,
        out_specs=(pl.BlockSpec(memory_space=pltpu.HBM),) * 4,
        scratch_shapes=[pltpu.SemaphoreType.DMA((4,))],
    )(*(pltpu.with_memory_space_constraint(a, pltpu.VMEM) for a in (act, gx, gs, gn)))
    return act, gx, gs.T, gn.T


def solution(mesh):
    return jax.shard_map(
        per_device,
        mesh=mesh,
        in_specs=(
            P("feat", "dom"),
            P(None, "feat"),
            P(None, "feat"),
            P("feat", "dom"),
            P("dom", None),
            P("dom"),
            P("dom", None),
            P("dom"),
        ),
        out_specs=(P("feat", "dom"), P("feat", "dom"), P(None, "feat"), P(None, "feat")),
        check_vma=False,
    )
```
